256 devices in a mesh: outer: 8 (over x, core), inner: 32 (over y, z).
Axes of the slice: x: 4, y: 4, z: 8, core: 2. Of those that a mesh axis runs over, the one named last changes fastest.
Arguments:
- features: bfloat16 [1048576, 512], P(('outer', 'inner'))
- targets: bfloat16 [1048576, 256], P(('outer', 'inner'))
- signs: int32 [1048576], P(('outer', 'inner')), may hold values from 0 to 1
- picks: int32 [262144], P(('outer', 'inner')), may hold values from 0 to 4095, as said below
- routes: int32 [262144], P(('outer', 'inner')), may hold values from 0 to 31, as said below
Outputs:
- sketch: bfloat16 [262144, 768], P(('outer', 'inner'))
- weights: float32 [512, 256], replicated
- predictions: bfloat16 [1048576, 256], P(('outer', 'inner'))
The draws below stay inside these ranges and needn't reach their ends.
Inputs may be any that keep to these rules, and one draw needn't show every extreme that they name: `signs`: row sign is 2 s - 1. `picks`: the 1024 entries of one block are distinct positions of that block. `routes`: among the 1024 entries of one block every value occurs exactly 32 times.
All inputs are finite; a program needn't handle non-finite values.
Results may differ from the reference program's by a relative error of at most 0.003.
The reference program's roundings to bfloat16 on the way (of `rows`, `kept` and `sectioned`) count: a program that leaves them out, or rounds other values in their place, can miss the bound.
Values may be sent and summed in bfloat16 or wider, within the bound.
A program may use at most 64 MiB of HBM per device.

```python
import math
import jax
import jax.numpy as jnp
from jax import lax

F = 512
K = 256
SIDE = 64
BLOCK = 4096
KEEP = 1024
INNER_RANKS = 32
NBLOCKS = 256
ROWS = 1048576
SKETCH = 262144
N_OUTER = 8
N_INNER = 32


def common_rows(key):
    key_base = jax.random.fold_in(key, 0)
    key_first = jax.random.fold_in(key, 2)
    key_second = jax.random.fold_in(key, 3)
    key_noise = jax.random.fold_in(key, 4)
    drawn = jax.random.normal(key_base, (ROWS, F), jnp.float32)
    base = drawn
    block_index = (jnp.arange(ROWS, dtype=jnp.int32) // BLOCK).astype(jnp.float32)
    rising = jnp.exp(math.log(4.0) * block_index / (NBLOCKS - 1))
    scale = rising[:, None]
    feats = base * scale
    first = jax.random.uniform(key_first, (NBLOCKS, K), jnp.float32, -1.2, 1.2) + 0.5
    second = jax.random.uniform(key_second, (NBLOCKS, K), jnp.float32, -1.2, 1.2) - 0.5
    first_rows = jnp.repeat(first, BLOCK, axis=0)
    second_rows = jnp.repeat(second, BLOCK, axis=0)
    noise = 0.6 * jax.random.normal(key_noise, (ROWS, K), jnp.float32) * scale
    goals = first_rows * feats[:, :K] + second_rows * feats[:, K:2 * K] + noise
    return (feats, goals)


def draw_features(key, part):
    feats, goals = common_rows(key)
    return feats.astype(jnp.bfloat16)


def draw_targets(key, part):
    feats, goals = common_rows(key)
    return goals.astype(jnp.bfloat16)


def draw_picks(key, part):
    key = jax.random.fold_in(key, 3)
    keys = jax.random.split(key, NBLOCKS)
    chosen = jax.vmap(lambda one: jax.random.permutation(one, BLOCK)[:KEEP])(keys)
    return chosen.reshape(-1).astype(jnp.int32)


def draw_routes(key, part):
    key = jax.random.fold_in(key, 5)
    keys = jax.random.split(key, NBLOCKS)
    base = (jnp.arange(KEEP, dtype=jnp.int32) % INNER_RANKS).astype(jnp.int32)
    shuffled = jax.vmap(lambda one: jax.random.permutation(one, base))(keys)
    return shuffled.reshape(-1).astype(jnp.int32)


def with_ends(array, key, smallest, high):
    longest = array.shape.index(max(array.shape))
    spots = []
    for shift in (0, 1):
        where = [jax.random.randint(jax.random.fold_in(key, axis), (), 0, length) for axis, length in enumerate(array.shape)]
        where[longest] = (where[longest] + shift) % array.shape[longest]
        spots.append(tuple(where))
    return array.at[spots[0]].set(smallest).at[spots[1]].set(high)


def setup_inputs(seed: int = 0) -> dict:
    key_of = jax.random.split(jax.random.key(seed), 6)
    return {
        "features": draw_features(jax.random.fold_in(key_of[5], 71), 0),
        "targets": draw_targets(jax.random.fold_in(key_of[5], 71), 0),
        "signs": with_ends(jax.random.randint(key_of[2], (ROWS,), 0, 2), jax.random.fold_in(key_of[2], 1), 0, 1).astype(jnp.int32),
        "picks": draw_picks(jax.random.fold_in(key_of[5], 71), 0),
        "routes": draw_routes(jax.random.fold_in(key_of[5], 71), 0),
    }


def hadamard(order):
    matrix = jnp.ones((1, 1), jnp.float32)
    while matrix.shape[0] < order:
        matrix = jnp.concatenate([jnp.concatenate([matrix, matrix], 1), jnp.concatenate([matrix, -matrix], 1)], 0)
    return matrix

def reference(features, targets, signs, picks, routes):
    width = F + K
    count = N_OUTER * N_INNER
    per_peer = KEEP // N_INNER
    factor = hadamard(SIDE)
    rows = jnp.concatenate([features, targets], 1).reshape(count, BLOCK, width)
    flips = (2 * signs - 1).astype(jnp.bfloat16).reshape(count, BLOCK, 1)
    chosen = picks.reshape(count, KEEP)

    def one_block(args):
        block, flip, keep_rows = args
        cube = (block * flip).astype(jnp.float32).reshape(SIDE, SIDE, width)
        half = jnp.einsum('bj,ijc->ibc', factor, cube, precision=lax.Precision.HIGHEST)
        whole = jnp.einsum('ai,ibc->abc', factor, half, precision=lax.Precision.HIGHEST) / SIDE
        return whole.reshape(BLOCK, width)[keep_rows].astype(jnp.bfloat16)
    kept = lax.map(one_block, (rows, flips, chosen))
    order = jnp.argsort(routes.reshape(count, KEEP), axis=1, stable=True)
    sectioned = jnp.take_along_axis(kept, order[:, :, None], axis=1)
    sectioned = sectioned.reshape(N_OUTER, N_INNER, N_INNER, per_peer, width)
    mixer = hadamard(N_INNER)
    mixed = jnp.einsum('rs,osdtc->odrtc', mixer, sectioned.astype(jnp.float32), precision=lax.Precision.HIGHEST) / math.sqrt(N_INNER)
    sketch = mixed.astype(jnp.bfloat16).reshape(SKETCH, width)
    gram = jnp.dot(sketch[:, :F].T.astype(jnp.float32), sketch.astype(jnp.float32), preferred_element_type=jnp.float32)
    lower = jnp.linalg.cholesky(gram[:, :F])
    middle = lax.linalg.triangular_solve(lower, gram[:, F:], left_side=True, lower=True)
    weights = lax.linalg.triangular_solve(lower, middle, left_side=True, lower=True, transpose_a=True)
    narrow = weights.astype(jnp.bfloat16)

    def predict(block):
        return jnp.dot(block.astype(jnp.float32), narrow.astype(jnp.float32), preferred_element_type=jnp.float32).astype(jnp.bfloat16)
    predictions = lax.map(predict, features.reshape(count, BLOCK, F)).reshape(ROWS, K)
    return (sketch, weights, predictions)
```

```python
import functools
import math

import jax
import jax.numpy as jnp
from jax import lax
from jax.experimental import pallas as pl
from jax.experimental.pallas import tpu as pltpu
from jax.sharding import PartitionSpec as P

F = 512
K = 256
BLOCK = 4096
KEEP = 1024
INNER = 32
NX, NC, NY, NZ = 4, 2, 4, 8
SECTION = KEEP // INNER
TILE = 128
G_BLOCKS = [(i, j) for i in range(4) for j in range(i, 4)]
R_BLOCKS = [(i, j) for i in range(4) for j in range(4, 6)]
G_ROWS = TILE * len(G_BLOCKS)
R_ROWS = TILE * len(R_BLOCKS)
HIGHEST = lax.Precision.HIGHEST
MESH = pl.DeviceIdType.MESH

NN = (((1,), (0,)), ((), ()))
NT = (((1,), (1,)), ((), ()))
TN = (((0,), (0,)), ((), ()))


def dot(a, b, dims=NN, precision=None):
    return lax.dot_general(a, b, dims, precision=precision, preferred_element_type=jnp.float32)


def iota(shape, dim):
    return lax.broadcasted_iota(jnp.int32, shape, dim)


def parity_sign(bits):
    bits = bits ^ (bits >> 8)
    bits = bits ^ (bits >> 4)
    bits = bits ^ (bits >> 2)
    bits = bits ^ (bits >> 1)
    return (1 - 2 * (bits & 1)).astype(jnp.float32)


def position(inner):
    return inner // NZ, lax.rem(inner, NZ)


def order_picks(picks_ref, routes_ref, upper_ref, coded_ref, factors_ref):
    picks = picks_ref[...]
    routes = routes_ref[...]

    @pl.loop(0, KEEP // TILE)
    def _(c):
        at = pl.multiple_of(c * TILE, TILE)
        row = iota((TILE, KEEP), 0) + at
        upper_ref[pl.ds(at, TILE), :] = (row < iota((TILE, KEEP), 1)).astype(jnp.float32).astype(jnp.bfloat16)

    hot = (iota((INNER, KEEP), 0) == routes).astype(jnp.float32)
    before = dot(hot.astype(jnp.bfloat16), upper_ref[...])
    rank = jnp.sum(hot * before, axis=0, keepdims=True)
    place = routes * SECTION + rank.astype(jnp.int32)
    low = iota((TILE, KEEP), 0) & picks
    coded_ref[pl.ds(0, TILE), :] = parity_sign(low).astype(jnp.bfloat16)
    for bit in range(5):
        high = 1 - 2 * ((picks >> (7 + bit)) & 1)
        coded_ref[pl.ds((bit + 1) * TILE, TILE), :] = jnp.broadcast_to(
            high.astype(jnp.float32), (TILE, KEEP)
        ).astype(jnp.bfloat16)

    @pl.loop(0, KEEP // TILE)
    def _(c):
        at = pl.multiple_of(c * TILE, TILE)
        chosen = (iota((TILE, KEEP), 0) + at == place).astype(jnp.float32).astype(jnp.bfloat16)
        factors_ref[pl.ds(at, TILE), :] = dot(chosen, coded_ref[...], NT).astype(jnp.bfloat16)


def fill_signs(signs_ref, flips_ref):
    for q in range(BLOCK // TILE):
        row = (2 * signs_ref[q : q + 1, :] - 1).astype(jnp.float32)
        flips_ref[:, q * TILE : (q + 1) * TILE] = jnp.broadcast_to(row, (16, TILE)).astype(jnp.bfloat16)


def fill_mixer(factors_ref, flips_ref, mixer_ref):
    rows = 64

    @pl.loop(0, KEEP // rows)
    def _(c):
        at = pl.multiple_of(c * rows, rows)
        here = factors_ref[pl.ds(at, rows), 0:TILE]
        gray = 0
        for step in range(BLOCK // TILE):
            if step:
                bit = (step & -step).bit_length() - 1
                gray ^= 1 << bit
                here = here * factors_ref[pl.ds(at, rows), (bit + 1) * TILE : (bit + 2) * TILE]
            flip = flips_ref[:, gray * TILE : (gray + 1) * TILE]
            flip = jnp.concatenate([flip] * (rows // 16), 0)
            mixer_ref[pl.ds(at, rows), gray * TILE : (gray + 1) * TILE] = here * flip


class Part:
    def __init__(self, rows, own, core_in, x_in, y_in, z_in, total, send, recv):
        self.rows = rows
        self.own, self.total = own, total
        self.core_in, self.x_in, self.y_in, self.z_in = core_in, x_in, y_in, z_in
        self.send, self.recv = send, recv
        outer = lax.axis_index("outer")
        self.x, self.core = outer // NC, lax.rem(outer, NC)
        self.y, self.z = position(lax.axis_index("inner"))
        self.half, self.eighth, self.piece = rows // 2, rows // 8, rows // 32
        self.at_half = pl.multiple_of(self.core * self.half, 8)
        self.at_eighth = pl.multiple_of(self.at_half + self.x * self.eighth, 8)
        self.at_piece = pl.multiple_of(self.at_eighth + self.y * self.piece, 8)
        self.copies = {}

    def copy(self, src, dst, slot_out, slot_in, device):
        return pltpu.make_async_remote_copy(
            src_ref=src,
            dst_ref=dst,
            send_sem=self.send.at[slot_out],
            recv_sem=self.recv.at[slot_in],
            device_id=device,
            device_id_type=MESH,
        )

    def start(self, stage):
        copies = []
        if stage == 0:
            other = 1 - self.core
            at = pl.multiple_of(other * self.half, 8)
            copies.append(self.copy(self.own.at[pl.ds(at, self.half)], self.core_in, 0, 0, {"outer": self.x * NC + other}))
        elif stage == 1:
            for d in range(1, NX):
                to = lax.rem(self.x + d, NX)
                at = pl.multiple_of(self.at_half + to * self.eighth, 8)
                copies.append(self.copy(self.own.at[pl.ds(at, self.eighth)], self.x_in.at[d - 1], d, d, {"outer": to * NC + self.core}))
        elif stage == 2:
            for d in range(1, NY):
                to = lax.rem(self.y + d, NY)
                at = pl.multiple_of(self.at_eighth + to * self.piece, 8)
                copies.append(self.copy(self.own.at[pl.ds(at, self.piece)], self.y_in.at[d - 1], 3 + d, 3 + d, {"inner": to * NZ + self.z}))
        elif stage == 3:
            for d in range(1, NZ):
                to = lax.rem(self.z + d, NZ)
                copies.append(
                    self.copy(self.own.at[pl.ds(self.at_piece, self.piece)], self.z_in.at[self.z], 6 + d, 6 + d, {"inner": self.y * NZ + to})
                )
        elif stage == 4:
            for d in range(1, NY):
                to = lax.rem(self.y + d, NY)
                where = self.total.at[pl.ds(self.at_piece, self.piece)]
                copies.append(self.copy(where, where, 13 + d, 13 + d, {"inner": to * NZ + self.z}))
        elif stage == 5:
            for d in range(1, NX):
                to = lax.rem(self.x + d, NX)
                where = self.total.at[pl.ds(self.at_eighth, self.eighth)]
                copies.append(self.copy(where, where, 16 + d, 16 + d, {"outer": to * NC + self.core}))
        else:
            where = self.total.at[pl.ds(self.at_half, self.half)]
            copies.append(self.copy(where, where, 20, 20, {"outer": self.x * NC + 1 - self.core}))
        for c in copies:
            c.start()
        self.copies[stage] = copies

    def finish(self, stage):
        if stage == 3:
            mine = self.own[pl.ds(self.at_piece, self.piece), :]
            self.z_in[self.z] = mine
        for c in self.copies[stage]:
            c.wait()
        if stage == 0:
            at = pl.ds(self.at_half, self.half)
            self.own[at, :] = self.own[at, :] + self.core_in[...]
        elif stage == 1:
            at = pl.ds(self.at_eighth, self.eighth)
            self.own[at, :] = (self.own[at, :] + self.x_in[0]) + (self.x_in[1] + self.x_in[2])
        elif stage == 2:
            at = pl.ds(self.at_piece, self.piece)
            self.own[at, :] = (self.own[at, :] + self.y_in[0]) + (self.y_in[1] + self.y_in[2])
        elif stage == 3:
            t = [self.z_in[i] for i in range(NZ)]
            t = [t[0] + t[1], t[2] + t[3], t[4] + t[5], t[6] + t[7]]
            self.total[pl.ds(self.at_piece, self.piece), :] = (t[0] + t[1]) + (t[2] + t[3])


SEMS = 21


def sketch_kernel(
    features, targets, signs_ref, picks_ref, routes_ref,
    sketch_ref, g_total, r_total,
    feat, targ, upper, coded, factors, flips, mixer,
    out_f, out_k, in_f, in_k,
    g_own, g_core, g_x, g_y, g_z,
    r_own, r_core, r_x, r_y, r_z,
    load_sem, own_sem, send_sem, recv_sem, g_send, g_recv, r_send, r_recv,
):
    outer = lax.axis_index("outer")
    me = lax.axis_index("inner")
    x, core = outer // NC, lax.rem(outer, NC)
    y, _ = position(me)

    loads = [
        pltpu.make_async_copy(features, feat, load_sem.at[0]),
        pltpu.make_async_copy(targets, targ, load_sem.at[1]),
    ]
    for load in loads:
        load.start()

    barrier = pltpu.get_barrier_semaphore()

    @pl.loop(1, INNER)
    def _(d):
        pl.semaphore_signal(barrier, inc=1, device_id={"inner": lax.rem(me + d, INNER)}, device_id_type=MESH)

    pl.semaphore_signal(barrier, inc=1, device_id={"outer": x * NC + 1 - core}, device_id_type=MESH)
    for d in range(1, NX):
        pl.semaphore_signal(barrier, inc=1, device_id={"outer": lax.rem(x + d, NX) * NC + core}, device_id_type=MESH)

    order_picks(picks_ref, routes_ref, upper, coded, factors)
    fill_signs(signs_ref, flips)
    fill_mixer(factors, flips, mixer)
    for load in loads:
        load.wait()
    pl.semaphore_wait(barrier, INNER - 1 + 1 + NX - 1)

    def section(ref, d):
        return ref.at[pl.ds(pl.multiple_of(d * SECTION, SECTION), SECTION)]

    def exchange(kind, out, into, d):
        return pltpu.make_async_remote_copy(
            src_ref=section(out, d),
            dst_ref=section(into, me),
            send_sem=send_sem.at[kind, d],
            recv_sem=recv_sem.at[kind, me],
            device_id={"inner": d},
            device_id_type=MESH,
        )

    span = NZ * SECTION
    for kind, (data, out, into) in enumerate([(feat, out_f, in_f), (targ, out_k, in_k)]):

        @pl.loop(0, NY)
        def _(c):
            row = lax.rem(y + c + 1, NY)
            at = pl.multiple_of(row * span, span)
            kept = dot(mixer[pl.ds(at, span), :], data[...])
            out[pl.ds(at, span), :] = (kept * (1.0 / 64)).astype(jnp.bfloat16)

            @pl.loop(0, NZ)
            def _(i):
                d = row * NZ + lax.rem(me + i + 1, NZ)

                @pl.when(d != me)
                def _():
                    exchange(kind, out, into, d).start()

    own = [
        pltpu.make_async_copy(section(out_f, me), section(in_f, me), own_sem.at[0]),
        pltpu.make_async_copy(section(out_k, me), section(in_k, me), own_sem.at[1]),
    ]
    for copy in own:
        copy.start()

    @pl.loop(0, KEEP // TILE)
    def _(c):
        at = pl.multiple_of(c * TILE, TILE)
        a = iota((TILE, KEEP), 0) + at
        b = iota((TILE, KEEP), 1)
        sign = parity_sign((a // SECTION) & (b // SECTION))
        upper[pl.ds(at, TILE), :] = jnp.where((a ^ b) & (SECTION - 1) == 0, sign, 0.0).astype(jnp.bfloat16)

    def arrive(kind, out, into):
        own[kind].wait()

        @pl.loop(1, INNER)
        def _(i):
            s = lax.rem(me + i, INNER)
            pltpu.make_async_remote_copy(
                src_ref=section(out, s),
                dst_ref=section(into, s),
                send_sem=send_sem.at[kind, s],
                recv_sem=recv_sem.at[kind, s],
                device_id={"inner": s},
                device_id_type=MESH,
            ).wait()

    def mix(into, first, width):
        @pl.loop(0, KEEP // 256)
        def _(c):
            at = pl.multiple_of(c * 256, 256)
            mixed = dot(upper[pl.ds(at, 256), :], into[...])
            sketch_ref[pl.ds(at, 256), first : first + width] = (mixed * (1.0 / math.sqrt(INNER))).astype(jnp.bfloat16)

    g = Part(G_ROWS, g_own, g_core, g_x, g_y, g_z, g_total, g_send, g_recv)
    r = Part(R_ROWS, r_own, r_core, r_x, r_y, r_z, r_total, r_send, r_recv)

    arrive(0, out_f, in_f)
    mix(in_f, 0, F)
    for i in range(4):
        rows = dot(sketch_ref[:, i * TILE : (i + 1) * TILE], sketch_ref[:, i * TILE : F], TN)
        for j in range(i, 4):
            at = G_BLOCKS.index((i, j)) * TILE
            g_own[at : at + TILE, :] = rows[:, (j - i) * TILE : (j - i + 1) * TILE]
    g.start(0)
    g.finish(0)
    g.start(1)
    g.finish(1)
    g.start(2)
    arrive(1, out_k, in_k)
    mix(in_k, F, K)
    for i in range(4):
        rows = dot(sketch_ref[:, i * TILE : (i + 1) * TILE], sketch_ref[:, F:], TN)
        for j in range(4, 6):
            at = R_BLOCKS.index((i, j)) * TILE
            r_own[at : at + TILE, :] = rows[:, (j - 4) * TILE : (j - 3) * TILE]
    r.start(0)
    for stage in range(2, 7):
        g.finish(stage)
        if stage < 6:
            g.start(stage + 1)
        r.finish(stage - 2)
        r.start(stage - 1)
    r.finish(5)
    r.start(6)
    r.finish(6)


def sketch_and_gram(features, targets, signs, picks, routes):
    vmem = pl.BlockSpec(memory_space=pltpu.VMEM)
    hbm = pl.BlockSpec(memory_space=pl.ANY)
    f32, bf16 = jnp.float32, jnp.bfloat16

    def part(rows):
        return [
            pltpu.VMEM((rows, TILE), f32),
            pltpu.VMEM((rows // 2, TILE), f32),
            pltpu.VMEM((NX - 1, rows // 8, TILE), f32),
            pltpu.VMEM((NY - 1, rows // 32, TILE), f32),
            pltpu.VMEM((NZ, rows // 32, TILE), f32),
        ]

    dma = pltpu.SemaphoreType.DMA
    return pl.pallas_call(
        sketch_kernel,
        out_shape=(
            jax.ShapeDtypeStruct((KEEP, F + K), bf16),
            jax.ShapeDtypeStruct((G_ROWS, TILE), f32),
            jax.ShapeDtypeStruct((R_ROWS, TILE), f32),
        ),
        in_specs=[hbm, hbm, vmem, vmem, vmem],
        out_specs=(vmem, vmem, vmem),
        scratch_shapes=[
            pltpu.VMEM((BLOCK, F), bf16),
            pltpu.VMEM((BLOCK, K), bf16),
            pltpu.VMEM((KEEP, KEEP), bf16),
            pltpu.VMEM((6 * TILE, KEEP), bf16),
            pltpu.VMEM((KEEP, 6 * TILE), bf16),
            pltpu.VMEM((16, BLOCK), bf16),
            pltpu.VMEM((KEEP, BLOCK), bf16),
            pltpu.VMEM((KEEP, F), bf16),
            pltpu.VMEM((KEEP, K), bf16),
            pltpu.VMEM((KEEP, F), bf16),
            pltpu.VMEM((KEEP, K), bf16),
        ]
        + part(G_ROWS)
        + part(R_ROWS)
        + [
            dma((2,)), dma((2,)), dma((2, INNER)), dma((2, INNER)),
            dma((SEMS,)), dma((SEMS,)), dma((SEMS,)), dma((SEMS,)),
        ],
        compiler_params=pltpu.CompilerParams(
            collective_id=0, has_side_effects=True, vmem_limit_bytes=56 << 20
        ),
        name="sketch",
    )(features, targets, signs, picks, routes)


def invert(block):
    lane = iota((8, TILE), 1)
    sub = iota((8, TILE), 0)

    def spread(v, j):
        return jnp.broadcast_to(v[:, j : j + 1], (8, TILE))

    def down(v, i):
        return jnp.broadcast_to(v[i : i + 1, :], (8, TILE))

    v = [block[8 * i : 8 * i + 8, :] for i in range(16)]
    for g in range(16):
        base = 8 * g
        now = v[g]
        cols = [spread(now, base + j) for j in range(8)]
        for s in range(8):
            over = 1.0 / down(cols[s], s)
            mult = jnp.where(sub == s, 0.0, cols[s])
            row = jnp.where(lane == base + s, 1.0, down(now, s)) * over
            now = jnp.where(sub == s, row, jnp.where(lane == base + s, 0.0, now) - mult * row)
            for j in range(s + 1, 8):
                pivot = down(cols[j], s) * over
                cols[j] = jnp.where(sub == s, pivot, cols[j] - mult * pivot)
        rows = [down(now, j) for j in range(8)]
        panel = (lane >= base) & (lane < base + 8)
        new = []
        for i in range(16):
            if i == g:
                new.append(now)
                continue
            p = [spread(v[i], base + j) * rows[j] for j in range(8)]
            p = ((p[0] + p[1]) + (p[2] + p[3])) + ((p[4] + p[5]) + (p[6] + p[7]))
            new.append(jnp.where(panel, 0.0, v[i]) - p)
        v = new
    return jnp.concatenate(v, 0)


def solve_kernel(features, g_ref, r_ref, weights_ref, predictions, feat, work, inverse, guess, load_sem, store_sem):
    load = pltpu.make_async_copy(features, feat, load_sem)
    load.start()
    for n, (i, j) in enumerate(G_BLOCKS):
        tile = g_ref[n * TILE : (n + 1) * TILE, :]
        work[i * TILE : (i + 1) * TILE, j * TILE : (j + 1) * TILE] = tile
        if i != j:
            work[j * TILE : (j + 1) * TILE, i * TILE : (i + 1) * TILE] = tile.T
    for n, (i, j) in enumerate(R_BLOCKS):
        work[i * TILE : (i + 1) * TILE, j * TILE : (j + 1) * TILE] = r_ref[n * TILE : (n + 1) * TILE, :]

    @pl.loop(0, F // TILE)
    def _(b):
        at = pl.multiple_of(b * TILE, TILE)
        inverse[...] = invert(work[pl.ds(at, TILE), pl.ds(at, TILE)])
        solved = dot(inverse[...], work[pl.ds(at, TILE), :], precision=HIGHEST)
        row = iota((F, TILE), 0)
        column = jnp.where((row >= at) & (row < at + TILE), 0.0, work[:, pl.ds(at, TILE)])
        work[...] = work[...] - dot(column, solved, precision=HIGHEST)
        work[pl.ds(at, TILE), :] = solved

    weights_ref[...] = work[:, F:]
    narrow = work[:, F:].astype(jnp.bfloat16)
    load.wait()
    chunk = BLOCK // 4
    stores = []
    for c in range(4):
        guess[c * chunk : (c + 1) * chunk, :] = dot(feat[c * chunk : (c + 1) * chunk, :], narrow).astype(jnp.bfloat16)
        store = pltpu.make_async_copy(
            guess.at[pl.ds(c * chunk, chunk)], predictions.at[pl.ds(c * chunk, chunk)], store_sem.at[c]
        )
        store.start()
        stores.append(store)
    for store in stores:
        store.wait()


def solve_and_predict(features, g_total, r_total):
    vmem = pl.BlockSpec(memory_space=pltpu.VMEM)
    hbm = pl.BlockSpec(memory_space=pl.ANY)
    return pl.pallas_call(
        solve_kernel,
        out_shape=(
            jax.ShapeDtypeStruct((F, K), jnp.float32),
            jax.ShapeDtypeStruct((BLOCK, K), jnp.bfloat16),
        ),
        in_specs=[hbm, vmem, vmem],
        out_specs=(vmem, hbm),
        scratch_shapes=[
            pltpu.VMEM((BLOCK, F), jnp.bfloat16),
            pltpu.VMEM((F, F + K), jnp.float32),
            pltpu.VMEM((TILE, TILE), jnp.float32),
            pltpu.VMEM((BLOCK, K), jnp.bfloat16),
            pltpu.SemaphoreType.DMA,
            pltpu.SemaphoreType.DMA((4,)),
        ],
        compiler_params=pltpu.CompilerParams(vmem_limit_bytes=40 << 20),
        name="solve",
    )(features, g_total, r_total)


def per_device(features, targets, signs, picks, routes):
    sketch, g_total, r_total = sketch_and_gram(
        features,
        targets,
        signs.reshape(BLOCK // TILE, TILE),
        picks.reshape(1, KEEP),
        routes.reshape(1, KEEP),
    )
    weights, predictions = solve_and_predict(features, g_total, r_total)
    return (sketch, weights, predictions)


def solution(mesh):
    both = ("outer", "inner")
    in_specs = (P(both, None), P(both, None), P(both), P(both), P(both))
    out_specs = (P(both, None), P(), P(both, None))
    return jax.shard_map(per_device, mesh=mesh, in_specs=in_specs, out_specs=out_specs, check_vma=False)
```

```python
import functools
import math

import jax
import jax.numpy as jnp
from jax import lax
from jax.experimental import pallas as pl
from jax.experimental.pallas import tpu as pltpu
from jax.sharding import PartitionSpec as P

F = 512
K = 256
BLOCK = 4096
KEEP = 1024
INNER = 32
NX, NC, NY, NZ = 4, 2, 4, 8
SECTION = KEEP // INNER
TILE = 128
G_BLOCKS = [(i, j) for i in range(4) for j in range(i, 4)]
R_BLOCKS = [(i, j) for i in range(4) for j in range(4, 6)]
G_ROWS = TILE * len(G_BLOCKS)
R_ROWS = TILE * len(R_BLOCKS)
HIGHEST = lax.Precision.HIGHEST
MESH = pl.DeviceIdType.MESH

NN = (((1,), (0,)), ((), ()))
NT = (((1,), (1,)), ((), ()))
TN = (((0,), (0,)), ((), ()))


def dot(a, b, dims=NN, precision=None):
    return lax.dot_general(a, b, dims, precision=precision, preferred_element_type=jnp.float32)


def iota(shape, dim):
    return lax.broadcasted_iota(jnp.int32, shape, dim)


def parity_sign(bits):
    bits = bits ^ (bits >> 8)
    bits = bits ^ (bits >> 4)
    bits = bits ^ (bits >> 2)
    bits = bits ^ (bits >> 1)
    return (1 - 2 * (bits & 1)).astype(jnp.float32)


def position(inner):
    return inner // NZ, lax.rem(inner, NZ)


def order_picks(small_ref, upper_ref, coded_ref, factors_ref):
    first = BLOCK // TILE

    def row_of(first):
        return jnp.concatenate([small_ref[first + i : first + i + 1, :] for i in range(KEEP // TILE)], 1)

    picks = row_of(first)
    routes = row_of(first + KEEP // TILE)

    @pl.loop(0, KEEP // TILE)
    def _(c):
        at = pl.multiple_of(c * TILE, TILE)
        row = iota((TILE, KEEP), 0) + at
        upper_ref[pl.ds(at, TILE), :] = (row < iota((TILE, KEEP), 1)).astype(jnp.float32).astype(jnp.bfloat16)

    hot = (iota((INNER, KEEP), 0) == routes).astype(jnp.float32)
    before = dot(hot.astype(jnp.bfloat16), upper_ref[...])
    rank = jnp.sum(hot * before, axis=0, keepdims=True)
    place = routes * SECTION + rank.astype(jnp.int32)
    for n, part in enumerate((picks & (TILE - 1), picks >> 7)):
        coded_ref[n * TILE : (n + 1) * TILE, :] = jnp.broadcast_to(
            part.astype(jnp.float32), (TILE, KEEP)
        ).astype(jnp.bfloat16)

    @pl.loop(0, KEEP // TILE)
    def _(c):
        at = pl.multiple_of(c * TILE, TILE)
        chosen = (iota((TILE, KEEP), 0) + at == place).astype(jnp.float32).astype(jnp.bfloat16)
        found = dot(chosen, coded_ref[...], NT).astype(jnp.int32)
        low = found[:, :TILE] & iota((TILE, TILE), 1)
        factors_ref[pl.ds(at, TILE), :TILE] = parity_sign(low).astype(jnp.bfloat16)
        for bit in range(5):
            high = 1 - 2 * ((found[:, TILE:] >> bit) & 1)
            factors_ref[pl.ds(at, TILE), (bit + 1) * TILE : (bit + 2) * TILE] = high.astype(jnp.float32).astype(jnp.bfloat16)


def fill_signs(signs_ref, flips_ref):
    for q in range(BLOCK // TILE):
        row = (2 * signs_ref[q : q + 1, :] - 1).astype(jnp.float32)
        flips_ref[:, q * TILE : (q + 1) * TILE] = jnp.broadcast_to(row, (16, TILE)).astype(jnp.bfloat16)


def fill_mixer(factors_ref, flips_ref, mixer_ref):
    rows = 64

    @pl.loop(0, KEEP // rows)
    def _(c):
        at = pl.multiple_of(c * rows, rows)
        here = factors_ref[pl.ds(at, rows), 0:TILE]
        gray = 0
        for step in range(BLOCK // TILE):
            if step:
                bit = (step & -step).bit_length() - 1
                gray ^= 1 << bit
                here = here * factors_ref[pl.ds(at, rows), (bit + 1) * TILE : (bit + 2) * TILE]
            flip = flips_ref[:, gray * TILE : (gray + 1) * TILE]
            flip = jnp.concatenate([flip] * (rows // 16), 0)
            mixer_ref[pl.ds(at, rows), gray * TILE : (gray + 1) * TILE] = here * flip


SIZES = {"core": NC, "x": NX, "y": NY, "z": NZ}


def flow_scratch(rows, stages):
    shapes, count = [], 0
    for kind, axis in stages:
        n = SIZES[axis]
        count += n - 1
        if kind == "scatter":
            rows //= n
            shapes.append((n - 1, rows, TILE))
        elif kind == "exchange":
            shapes.append((n, rows, TILE))
        else:
            rows *= n
    return shapes, count


class Flow:
    def __init__(self, own, total, first, rows, stages, landing, send, recv):
        self.own, self.total, self.at, self.rows = own, total, first, rows
        self.stages, self.landing, self.send, self.recv = list(stages), list(landing), send, recv
        self.slot = 0
        self.exchanges_left = sum(kind == "exchange" for kind, _ in stages)
        outer = lax.axis_index("outer")
        inner = lax.axis_index("inner")
        self.place = {"x": outer // NC, "core": lax.rem(outer, NC), "y": inner // NZ, "z": lax.rem(inner, NZ)}

    def device(self, axis, to):
        p = self.place
        if axis == "x":
            return {"outer": to * NC + p["core"]}
        if axis == "core":
            return {"outer": p["x"] * NC + to}
        if axis == "y":
            return {"inner": to * NZ + p["z"]}
        return {"inner": p["y"] * NZ + to}

    def start(self):
        kind, axis = self.stages.pop(0)
        n, me = SIZES[axis], self.place[axis]
        buffer = None if kind == "gather" else self.landing.pop(0)
        copies = []
        for d in range(1, n):
            to = lax.rem(me + d, n)
            if kind == "scatter":
                piece = self.rows // n
                src = self.own.at[pl.ds(pl.multiple_of(self.at + to * piece, 8), piece)]
                dst = buffer.at[d - 1]
            elif kind == "exchange":
                src = self.own.at[pl.ds(pl.multiple_of(self.at, 8), self.rows)]
                dst = buffer.at[me]
            else:
                src = dst = self.total.at[pl.ds(pl.multiple_of(self.at, 8), self.rows)]
            copies.append(
                pltpu.make_async_remote_copy(
                    src_ref=src,
                    dst_ref=dst,
                    send_sem=self.send.at[self.slot],
                    recv_sem=self.recv.at[self.slot],
                    device_id=self.device(axis, to),
                    device_id_type=MESH,
                )
            )
            self.slot += 1
        for copy in copies:
            copy.start()
        self.flight = kind, axis, buffer, copies

    def finish(self):
        kind, axis, buffer, copies = self.flight
        n, me = SIZES[axis], self.place[axis]
        if kind == "exchange":
            buffer[me] = self.own[pl.ds(pl.multiple_of(self.at, 8), self.rows), :]
        for copy in copies:
            copy.wait()
        if kind == "scatter":
            self.rows //= n
            self.at = self.at + me * self.rows
            where = pl.ds(pl.multiple_of(self.at, 8), self.rows)
            terms = [self.own[where, :]] + [buffer[i] for i in range(n - 1)]
        elif kind == "exchange":
            where = pl.ds(pl.multiple_of(self.at, 8), self.rows)
            terms = [buffer[i] for i in range(n)]
        else:
            self.at = self.at - me * self.rows
            self.rows *= n
            return
        while len(terms) > 1:
            terms = [terms[i] + terms[i + 1] for i in range(0, len(terms), 2)]
        self.exchanges_left -= kind == "exchange"
        into = self.own if self.exchanges_left else self.total
        into[where, :] = terms[0]

    def step(self):
        if getattr(self, "flight", None):
            self.finish()
            self.flight = None
        if self.stages:
            self.start()

    def done(self):
        return not self.stages and self.flight is None


CORE = [("scatter", "core")]
FLOW_X = [("scatter", "x"), ("scatter", "y"), ("exchange", "z"), ("gather", "y"), ("gather", "x")]
FLOW_Y = [("scatter", "y"), ("scatter", "x"), ("exchange", "z"), ("gather", "x"), ("gather", "y")]
FLOW_Z = [("scatter", "z"), ("exchange", "x"), ("exchange", "y"), ("gather", "z")]
G_FLOWS = [(256, FLOW_X), (256, FLOW_Y), (128, FLOW_Z)]
R_FLOWS = [(256, FLOW_X), (256, FLOW_Y)]


class Sum:
    def __init__(self, own, total, rows, flows, landing, send, recv):
        self.core = Flow(own, total, 0, rows, CORE + [("gather", "core")], landing[:1], send, recv)
        self.core.exchanges_left = 1
        self.flows, self.args = None, (own, total, rows, flows, landing[1:], send, recv)
        self.phase = 0

    def step(self):
        if self.phase == 0:
            self.core.step()
        elif self.phase == 1:
            self.core.finish()
            self.core.flight = None
            own, total, rows, flows, landing, send, recv = self.args
            at, base, self.flows = self.core.at, 2, []
            for size, stages in flows:
                shapes, count = flow_scratch(size, stages)
                used = [landing.pop(0) for _ in shapes]
                flow = Flow(own, total, at, size, stages, used, send, recv)
                flow.slot = base
                base += count
                at = at + size
                flow.step()
                self.flows.append(flow)
        elif not all(flow.done() for flow in self.flows):
            for flow in self.flows:
                if not flow.done():
                    flow.step()
            if all(flow.done() for flow in self.flows):
                self.core.step()
        else:
            self.core.step()
            self.finished = True
        self.phase += 1

    finished = False


def sum_scratch(rows, flows):
    shapes, count = flow_scratch(rows, CORE)
    count += 1
    for size, stages in flows:
        more, n = flow_scratch(size, stages)
        shapes, count = shapes + more, count + n
    return shapes, count


def invert(block):
    lane = iota((8, TILE), 1)
    sub = iota((8, TILE), 0)

    def spread(v, j):
        return jnp.broadcast_to(v[:, j : j + 1], (8, TILE))

    def down(v, i):
        return jnp.broadcast_to(v[i : i + 1, :], (8, TILE))

    v = [block[8 * i : 8 * i + 8, :] for i in range(16)]
    for g in range(16):
        base = 8 * g
        now = v[g]
        cols = [spread(now, base + j) for j in range(8)]
        for s in range(8):
            over = 1.0 / down(cols[s], s)
            mult = jnp.where(sub == s, 0.0, cols[s])
            row = jnp.where(lane == base + s, 1.0, down(now, s)) * over
            now = jnp.where(sub == s, row, jnp.where(lane == base + s, 0.0, now) - mult * row)
            for j in range(s + 1, 8):
                pivot = down(cols[j], s) * over
                cols[j] = jnp.where(sub == s, pivot, cols[j] - mult * pivot)
        rows = [down(now, j) for j in range(8)]
        panel = (lane >= base) & (lane < base + 8)
        new = []
        for i in range(16):
            if i == g:
                new.append(now)
                continue
            p = [spread(v[i], base + j) * rows[j] for j in range(8)]
            p = ((p[0] + p[1]) + (p[2] + p[3])) + ((p[4] + p[5]) + (p[6] + p[7]))
            new.append(jnp.where(panel, 0.0, v[i]) - p)
        v = new
    return jnp.concatenate(v, 0)


def fill_kron(kron):
    @pl.loop(0, KEEP // TILE)
    def _(c):
        at = pl.multiple_of(c * TILE, TILE)
        a = iota((TILE, KEEP), 0) + at
        b = iota((TILE, KEEP), 1)
        sign = parity_sign((a // SECTION) & (b // SECTION))
        kron[pl.ds(at, TILE), :] = jnp.where((a ^ b) & (SECTION - 1) == 0, sign, 0.0).astype(jnp.bfloat16)


EARLY = {(0, 0), (0, 1)}


def sketch_kernel(
    features, targets, small_ref,
    sketch_hbm, weights_ref,
    feat, targ, upper, coded, factors, flips, mixer,
    out_f, out_k, in_f, in_k, sketch, work, inverse, g_own, g_total, r_own, r_total,
    load_sem, own_sem, store_sem, send_sem, recv_sem, g_send, g_recv, r_send, r_recv, *landing
):
    outer = lax.axis_index("outer")
    me = lax.axis_index("inner")
    x, core = outer // NC, lax.rem(outer, NC)
    y, _ = position(me)

    loads = [
        pltpu.make_async_copy(features, feat, load_sem.at[0]),
        pltpu.make_async_copy(targets, targ, load_sem.at[1]),
    ]
    for load in loads:
        load.start()

    barrier = pltpu.get_barrier_semaphore()

    @pl.loop(1, INNER)
    def _(d):
        pl.semaphore_signal(barrier, inc=1, device_id={"inner": lax.rem(me + d, INNER)}, device_id_type=MESH)

    pl.semaphore_signal(barrier, inc=1, device_id={"outer": x * NC + 1 - core}, device_id_type=MESH)
    for d in range(1, NX):
        pl.semaphore_signal(barrier, inc=1, device_id={"outer": lax.rem(x + d, NX) * NC + core}, device_id_type=MESH)

    order_picks(small_ref, upper, coded, factors)
    fill_signs(small_ref, flips)
    fill_mixer(factors, flips, mixer)
    pl.semaphore_wait(barrier, INNER - 1 + 1 + NX - 1)

    def section(ref, d):
        return ref.at[pl.ds(pl.multiple_of(d * SECTION, SECTION), SECTION)]

    pairs = [(feat, out_f, in_f), (targ, out_k, in_k)]

    def exchange(kind, to, source):
        _, out, into = pairs[kind]
        return pltpu.make_async_remote_copy(
            src_ref=section(out, to),
            dst_ref=section(into, source),
            send_sem=send_sem.at[kind, to],
            recv_sem=recv_sem.at[kind, source],
            device_id={"inner": to},
            device_id_type=MESH,
        )

    span = NZ * SECTION

    def keep(kind, c):
        data, out, _ = pairs[kind]
        at = pl.multiple_of(lax.rem(y + c + 1, NY) * span, span)
        kept = dot(mixer[pl.ds(at, span), :], data[...])
        out[pl.ds(at, span), :] = (kept * (1.0 / 64)).astype(jnp.bfloat16)

    def send(kind, c):
        row = lax.rem(y + c + 1, NY)

        @pl.loop(0, NZ)
        def _(i):
            to = row * NZ + lax.rem(me + i + 1, NZ)

            @pl.when(to != me)
            def _():
                exchange(kind, to, me).start()

    def make(kind):
        loads[kind].wait()
        early = [c for c in range(NY) if (kind, c) in EARLY]
        if early:
            assert early == list(range(len(early)))

            @pl.loop(0, len(early))
            def _(c):
                keep(kind, c)
                send(kind, c)

        @pl.loop(len(early), NY)
        def _(c):
            keep(kind, c)

    def send_rest(kind):
        late = [c for c in range(NY) if (kind, c) not in EARLY]

        @pl.loop(late[0], NY)
        def _(c):
            send(kind, c)

    def arrive(kind):
        own[kind].wait()

        @pl.loop(1, INNER)
        def _(i):
            s = lax.rem(me + i, INNER)
            exchange(kind, s, s).wait()

    def mix(kind):
        first, width = ((0, F), (F, K))[kind]
        into = pairs[kind][2]

        @pl.loop(0, KEEP // 256)
        def _(c):
            at = pl.multiple_of(c * 256, 256)
            mixed = dot(upper[pl.ds(at, 256), :], into[...])
            sketch[pl.ds(at, 256), first : first + width] = (mixed * (1.0 / math.sqrt(INNER))).astype(jnp.bfloat16)

    def eliminate(b, columns):
        at = b * TILE
        pivot = dot(inverse[b], work[at : at + TILE, columns], precision=HIGHEST)
        for first, last in ((0, at), (at + TILE, F)):
            if first < last:
                work[first:last, columns] = work[first:last, columns] - dot(
                    work[first:last, at : at + TILE], pivot, precision=HIGHEST
                )
        work[at : at + TILE, columns] = pivot

    count = len(landing) - len(sum_scratch(R_ROWS, R_FLOWS)[0])
    g = Sum(g_own, g_total, G_ROWS, G_FLOWS, list(landing[:count]), g_send, g_recv)
    r = Sum(r_own, r_total, R_ROWS, R_FLOWS, list(landing[count:]), r_send, r_recv)

    make(0)
    for i in (0, 2):
        rows = dot(out_f[:, i * TILE : (i + 2) * TILE], out_f[:, i * TILE :], TN)
        for n, (p, q) in enumerate(G_BLOCKS):
            if p in (i, i + 1):
                g_own[n * TILE : (n + 1) * TILE, :] = rows[(p - i) * TILE : (p - i + 1) * TILE, (q - i) * TILE : (q - i + 1) * TILE]
    g.step()
    make(1)
    own = [
        pltpu.make_async_copy(section(out_f, me), section(in_f, me), own_sem.at[0]),
        pltpu.make_async_copy(section(out_k, me), section(in_k, me), own_sem.at[1]),
    ]
    for copy in own:
        copy.start()
    g.step()
    for i in (0, 2):
        rows = dot(out_f[:, i * TILE : (i + 2) * TILE], out_k[...], TN)
        for n, (p, q) in enumerate(R_BLOCKS):
            if p in (i, i + 1):
                r_own[n * TILE : (n + 1) * TILE, :] = rows[(p - i) * TILE : (p - i + 1) * TILE, (q - 4) * TILE : (q - 3) * TILE]
    fill_kron(upper)
    g.step()
    r.step()
    while not g.finished:
        g.step()
        r.step()
    send_rest(0)
    send_rest(1)

    for n, (i, j) in enumerate(G_BLOCKS):
        tile = g_total[n * TILE : (n + 1) * TILE, :]
        work[i * TILE : (i + 1) * TILE, j * TILE : (j + 1) * TILE] = tile
        if i != j:
            work[j * TILE : (j + 1) * TILE, i * TILE : (i + 1) * TILE] = tile.T
    targets_at = slice(F, F + K)
    for b in range(F // TILE):
        at = b * TILE
        inverse[b] = invert(work[at : at + TILE, at : at + TILE])
        if b < 3:
            eliminate(b, slice(at + TILE, F))
        if not r.finished:
            r.step()
        if b == 1:
            while not r.finished:
                r.step()
            for n, (i, j) in enumerate(R_BLOCKS):
                work[i * TILE : (i + 1) * TILE, j * TILE : (j + 1) * TILE] = r_total[n * TILE : (n + 1) * TILE, :]
            eliminate(0, targets_at)
        if b:
            eliminate(b, targets_at)
        if b == 2:
            arrive(0)
            mix(0)
            arrive(1)
            mix(1)
            store = pltpu.make_async_copy(sketch, sketch_hbm, store_sem)
            store.start()
    weights_ref[...] = work[:, targets_at]
    store.wait()


def sketch_and_weights(features, targets, small):
    vmem = pl.BlockSpec(memory_space=pltpu.VMEM)
    hbm = pl.BlockSpec(memory_space=pl.ANY)
    f32, bf16 = jnp.float32, jnp.bfloat16
    dma = pltpu.SemaphoreType.DMA
    g_shapes, g_count = sum_scratch(G_ROWS, G_FLOWS)
    r_shapes, r_count = sum_scratch(R_ROWS, R_FLOWS)
    return pl.pallas_call(
        sketch_kernel,
        out_shape=(
            jax.ShapeDtypeStruct((KEEP, F + K), bf16),
            jax.ShapeDtypeStruct((F, K), f32),
        ),
        in_specs=[hbm, hbm, vmem],
        out_specs=(hbm, vmem),
        scratch_shapes=[
            pltpu.VMEM((BLOCK, F), bf16),
            pltpu.VMEM((BLOCK, K), bf16),
            pltpu.VMEM((KEEP, KEEP), bf16),
            pltpu.VMEM((2 * TILE, KEEP), bf16),
            pltpu.VMEM((KEEP, 6 * TILE), bf16),
            pltpu.VMEM((16, BLOCK), bf16),
            pltpu.VMEM((KEEP, BLOCK), bf16),
            pltpu.VMEM((KEEP, F), bf16),
            pltpu.VMEM((KEEP, K), bf16),
            pltpu.VMEM((KEEP, F), bf16),
            pltpu.VMEM((KEEP, K), bf16),
            pltpu.VMEM((KEEP, F + K), bf16),
            pltpu.VMEM((F, F + K), f32),
            pltpu.VMEM((F // TILE, TILE, TILE), f32),
            pltpu.VMEM((G_ROWS, TILE), f32),
            pltpu.VMEM((G_ROWS, TILE), f32),
            pltpu.VMEM((R_ROWS, TILE), f32),
            pltpu.VMEM((R_ROWS, TILE), f32),
            dma((2,)), dma((2,)), dma, dma((2, INNER)), dma((2, INNER)),
            dma((g_count,)), dma((g_count,)), dma((r_count,)), dma((r_count,)),
        ]
        + [pltpu.VMEM(shape, f32) for shape in g_shapes + r_shapes],
        compiler_params=pltpu.CompilerParams(
            collective_id=0, has_side_effects=True, vmem_limit_bytes=51 << 20
        ),
        name="sketch",
    )(features, targets, small)


def predict_kernel(feat, weights_in, sketch_in, sketch_ref, weights_ref, predictions, guess, copy_sem, store_sem):
    copy = pltpu.make_async_copy(sketch_in, sketch_ref, copy_sem)
    copy.start()
    weights_ref[...] = weights_in[...]
    narrow = weights_in[...].astype(jnp.bfloat16)
    chunk = BLOCK // 8
    stores = []
    for c in range(8):
        rows = slice(c * chunk, (c + 1) * chunk)
        guess[rows, :] = dot(feat[rows, :], narrow).astype(jnp.bfloat16)
        where = pl.ds(c * chunk, chunk)
        store = pltpu.make_async_copy(guess.at[where], predictions.at[where], store_sem.at[c])
        store.start()
        stores.append(store)
    for store in stores:
        store.wait()
    copy.wait()


def predict(features, weights, sketch):
    vmem = pl.BlockSpec(memory_space=pltpu.VMEM)
    hbm = pl.BlockSpec(memory_space=pl.ANY)
    return pl.pallas_call(
        predict_kernel,
        out_shape=(
            jax.ShapeDtypeStruct((KEEP, F + K), jnp.bfloat16),
            jax.ShapeDtypeStruct((F, K), jnp.float32),
            jax.ShapeDtypeStruct((BLOCK, K), jnp.bfloat16),
        ),
        in_specs=[vmem, vmem, hbm],
        out_specs=(hbm, vmem, hbm),
        scratch_shapes=[
            pltpu.VMEM((BLOCK, K), jnp.bfloat16),
            pltpu.SemaphoreType.DMA,
            pltpu.SemaphoreType.DMA((8,)),
        ],
        compiler_params=pltpu.CompilerParams(vmem_limit_bytes=12 << 20),
        name="predict",
    )(features, weights, sketch)


def per_device(features, targets, signs, picks, routes):
    sketch, weights = sketch_and_weights(
        features,
        targets,
        jnp.concatenate([signs, picks, routes]).reshape((BLOCK + 2 * KEEP) // TILE, TILE),
    )
    return predict(features, weights, sketch)


def solution(mesh):
    both = ("outer", "inner")
    in_specs = (P(both, None), P(both, None), P(both), P(both), P(both))
    out_specs = (P(both, None), P(), P(both, None))
    return jax.shard_map(per_device, mesh=mesh, in_specs=in_specs, out_specs=out_specs, check_vma=False)
```

```python
import functools
import math

import jax
import jax.numpy as jnp
from jax import lax
from jax.experimental import pallas as pl
from jax.experimental.pallas import tpu as pltpu
from jax.sharding import PartitionSpec as P

F = 512
K = 256
BLOCK = 4096
KEEP = 1024
INNER = 32
NX, NC, NY, NZ = 4, 2, 4, 8
SECTION = KEEP // INNER
TILE = 128
G_BLOCKS = [(i, j) for i in range(4) for j in range(i, 4)]
R_BLOCKS = [(i, j) for i in range(4) for j in range(4, 6)]
G_ROWS = TILE * len(G_BLOCKS)
R_ROWS = TILE * len(R_BLOCKS)
HIGHEST = lax.Precision.HIGHEST
MESH = pl.DeviceIdType.MESH

NN = (((1,), (0,)), ((), ()))
NT = (((1,), (1,)), ((), ()))
TN = (((0,), (0,)), ((), ()))


def dot(a, b, dims=NN, precision=None):
    return lax.dot_general(a, b, dims, precision=precision, preferred_element_type=jnp.float32)


def iota(shape, dim):
    return lax.broadcasted_iota(jnp.int32, shape, dim)


def parity_sign(bits):
    bits = bits ^ (bits >> 4)
    bits = bits ^ (bits >> 2)
    bits = bits ^ (bits >> 1)
    return (1 - 2 * (bits & 1)).astype(jnp.float32)


def position(inner):
    return inner // NZ, lax.rem(inner, NZ)


def order_picks(small_ref, upper_ref, coded_ref, factors_ref):
    first = BLOCK // TILE

    def row_of(first):
        return jnp.concatenate([small_ref[first + i : first + i + 1, :] for i in range(KEEP // TILE)], 1)

    picks = row_of(first)
    routes = row_of(first + KEEP // TILE)

    above = (iota((TILE, TILE), 0) < iota((TILE, TILE), 1)).astype(jnp.float32).astype(jnp.bfloat16)
    for q in range(KEEP // TILE):
        for p in range(KEEP // TILE):
            tile = above if p == q else jnp.full((TILE, TILE), float(p > q), jnp.bfloat16)
            upper_ref[q * TILE : (q + 1) * TILE, p * TILE : (p + 1) * TILE] = tile

    hot = (iota((INNER, KEEP), 0) == routes).astype(jnp.float32)
    before = dot(hot.astype(jnp.bfloat16), upper_ref[...])
    rank = jnp.sum(hot * before, axis=0, keepdims=True)
    place = routes * SECTION + rank.astype(jnp.int32)
    for n, part in enumerate((picks & (TILE - 1), picks >> 7)):
        coded_ref[n * TILE : (n + 1) * TILE, :] = jnp.broadcast_to(
            part.astype(jnp.float32), (TILE, KEEP)
        ).astype(jnp.bfloat16)

    rows = 2 * TILE

    @pl.loop(0, KEEP // rows)
    def _(c):
        at = pl.multiple_of(c * rows, rows)
        chosen = (iota((rows, KEEP), 0) + at == place).astype(jnp.float32).astype(jnp.bfloat16)
        found = dot(chosen, coded_ref[...], NT).astype(jnp.int32)
        low = found[:, :TILE] & iota((rows, TILE), 1)
        factors_ref[pl.ds(at, rows), :TILE] = parity_sign(low).astype(jnp.bfloat16)
        for bit in range(5):
            high = 1 - 2 * ((found[:, TILE:] >> bit) & 1)
            factors_ref[pl.ds(at, rows), (bit + 1) * TILE : (bit + 2) * TILE] = high.astype(jnp.float32).astype(jnp.bfloat16)


def fill_signs(signs_ref, flips_ref):
    for q in range(BLOCK // TILE):
        row = (2 * signs_ref[q : q + 1, :] - 1).astype(jnp.float32)
        flips_ref[:, q * TILE : (q + 1) * TILE] = jnp.broadcast_to(row, (16, TILE)).astype(jnp.bfloat16)


def fill_mixer(factors_ref, flips_ref, mixer_ref):
    rows = 64

    @pl.loop(0, KEEP // rows)
    def _(c):
        at = pl.multiple_of(c * rows, rows)
        here = factors_ref[pl.ds(at, rows), 0:TILE]
        gray = 0
        for step in range(BLOCK // TILE):
            if step:
                bit = (step & -step).bit_length() - 1
                gray ^= 1 << bit
                here = here * factors_ref[pl.ds(at, rows), (bit + 1) * TILE : (bit + 2) * TILE]
            flip = flips_ref[:, gray * TILE : (gray + 1) * TILE]
            flip = jnp.concatenate([flip] * (rows // 16), 0)
            mixer_ref[pl.ds(at, rows), gray * TILE : (gray + 1) * TILE] = here * flip


SIZES = {"core": NC, "x": NX, "y": NY, "z": NZ}


def flow_scratch(rows, stages):
    shapes, count = [], 0
    for kind, axis in stages:
        n = SIZES[axis]
        count += n - 1
        if kind == "scatter":
            rows //= n
            shapes.append((n - 1, rows, TILE))
        elif kind == "exchange":
            shapes.append((n, rows, TILE))
        else:
            rows *= n
    return shapes, count


class Flow:
    def __init__(self, own, total, first, rows, stages, landing, send, recv):
        self.own, self.total, self.at, self.rows = own, total, first, rows
        self.stages, self.landing, self.send, self.recv = list(stages), list(landing), send, recv
        self.slot = 0
        self.exchanges_left = sum(kind == "exchange" for kind, _ in stages)
        outer = lax.axis_index("outer")
        inner = lax.axis_index("inner")
        self.place = {"x": outer // NC, "core": lax.rem(outer, NC), "y": inner // NZ, "z": lax.rem(inner, NZ)}

    def device(self, axis, to):
        p = self.place
        if axis == "x":
            return {"outer": to * NC + p["core"]}
        if axis == "core":
            return {"outer": p["x"] * NC + to}
        if axis == "y":
            return {"inner": to * NZ + p["z"]}
        return {"inner": p["y"] * NZ + to}

    def start(self):
        kind, axis = self.stages.pop(0)
        n, me = SIZES[axis], self.place[axis]
        buffer = None if kind == "gather" else self.landing.pop(0)
        copies = []
        for d in range(1, n):
            to = lax.rem(me + d, n)
            if kind == "scatter":
                piece = self.rows // n
                src = self.own.at[pl.ds(pl.multiple_of(self.at + to * piece, 8), piece)]
                dst = buffer.at[d - 1]
            elif kind == "exchange":
                src = self.own.at[pl.ds(pl.multiple_of(self.at, 8), self.rows)]
                dst = buffer.at[me]
            else:
                src = dst = self.total.at[pl.ds(pl.multiple_of(self.at, 8), self.rows)]
            copies.append(
                pltpu.make_async_remote_copy(
                    src_ref=src,
                    dst_ref=dst,
                    send_sem=self.send.at[self.slot],
                    recv_sem=self.recv.at[self.slot],
                    device_id=self.device(axis, to),
                    device_id_type=MESH,
                )
            )
            self.slot += 1
        for copy in copies:
            copy.start()
        self.flight = kind, axis, buffer, copies

    def finish(self):
        kind, axis, buffer, copies = self.flight
        n, me = SIZES[axis], self.place[axis]
        if kind == "exchange":
            buffer[me] = self.own[pl.ds(pl.multiple_of(self.at, 8), self.rows), :]
        for copy in copies:
            copy.wait()
        if kind == "scatter":
            self.rows //= n
            self.at = self.at + me * self.rows
            where = pl.ds(pl.multiple_of(self.at, 8), self.rows)
            terms = [self.own[where, :]] + [buffer[i] for i in range(n - 1)]
        elif kind == "exchange":
            where = pl.ds(pl.multiple_of(self.at, 8), self.rows)
            terms = [buffer[i] for i in range(n)]
        else:
            self.at = self.at - me * self.rows
            self.rows *= n
            return
        while len(terms) > 1:
            terms = [terms[i] + terms[i + 1] for i in range(0, len(terms), 2)]
        self.exchanges_left -= kind == "exchange"
        into = self.own if self.exchanges_left else self.total
        into[where, :] = terms[0]

    def step(self):
        if getattr(self, "flight", None):
            self.finish()
            self.flight = None
        if self.stages:
            self.start()

    def done(self):
        return not self.stages and self.flight is None


CORE = [("scatter", "core")]
FLOW_X = [("scatter", "x"), ("scatter", "y"), ("exchange", "z"), ("gather", "y"), ("gather", "x")]
FLOW_Y = [("scatter", "y"), ("scatter", "x"), ("exchange", "z"), ("gather", "x"), ("gather", "y")]
G_FLOWS = [(384, FLOW_X), (256, FLOW_Y)]
R_FLOWS = [(256, FLOW_X), (256, FLOW_Y)]


class Sum:
    def __init__(self, own, total, rows, flows, landing, send, recv):
        self.core = Flow(own, total, 0, rows, CORE + [("gather", "core")], landing[:1], send, recv)
        self.core.exchanges_left = 1
        self.flows, self.args = None, (own, total, rows, flows, landing[1:], send, recv)
        self.phase = 0

    def step(self):
        if self.phase == 0:
            self.core.step()
        elif self.phase == 1:
            self.core.finish()
            self.core.flight = None
            own, total, rows, flows, landing, send, recv = self.args
            at, base, self.flows = self.core.at, 2, []
            for size, stages in flows:
                shapes, count = flow_scratch(size, stages)
                used = [landing.pop(0) for _ in shapes]
                flow = Flow(own, total, at, size, stages, used, send, recv)
                flow.slot = base
                base += count
                at = at + size
                flow.step()
                self.flows.append(flow)
        elif not all(flow.done() for flow in self.flows):
            for flow in self.flows:
                if not flow.done():
                    flow.step()
            if all(flow.done() for flow in self.flows):
                self.core.step()
        else:
            self.core.step()
            self.finished = True
        self.phase += 1

    finished = False


def sum_scratch(rows, flows):
    shapes, count = flow_scratch(rows, CORE)
    count += 1
    for size, stages in flows:
        more, n = flow_scratch(size, stages)
        shapes, count = shapes + more, count + n
    return shapes, count


def invert(block):
    lane = iota((8, TILE), 1)
    sub = iota((8, TILE), 0)

    def spread(v, j):
        return jnp.broadcast_to(v[:, j : j + 1], (8, TILE))

    def down(v, i):
        return jnp.broadcast_to(v[i : i + 1, :], (8, TILE))

    v = [block[8 * i : 8 * i + 8, :] for i in range(16)]
    for g in range(16):
        base = 8 * g
        now = v[g]
        cols = [spread(now, base + j) for j in range(8)]
        for s in range(8):
            over = 1.0 / down(cols[s], s)
            mult = jnp.where(sub == s, 0.0, cols[s])
            row = jnp.where(lane == base + s, 1.0, down(now, s)) * over
            now = jnp.where(sub == s, row, jnp.where(lane == base + s, 0.0, now) - mult * row)
            for j in range(s + 1, 8):
                pivot = down(cols[j], s) * over
                cols[j] = jnp.where(sub == s, pivot, cols[j] - mult * pivot)
        rows = [down(now, j) for j in range(8)]
        panel = (lane >= base) & (lane < base + 8)
        new = []
        for i in range(16):
            if i == g:
                new.append(now)
                continue
            p = [spread(v[i], base + j) * rows[j] for j in range(8)]
            p = ((p[0] + p[1]) + (p[2] + p[3])) + ((p[4] + p[5]) + (p[6] + p[7]))
            new.append(jnp.where(panel, 0.0, v[i]) - p)
        v = new
    return jnp.concatenate(v, 0)


def fill_kron(kron):
    a, b = iota((TILE, TILE), 0), iota((TILE, TILE), 1)
    sign = parity_sign((a // SECTION) & (b // SECTION))
    tile = jnp.where((a ^ b) & (SECTION - 1) == 0, sign, 0.0)
    tiles = [tile.astype(jnp.bfloat16), (-tile).astype(jnp.bfloat16)]
    for q in range(KEEP // TILE):
        for p in range(KEEP // TILE):
            kron[q * TILE : (q + 1) * TILE, p * TILE : (p + 1) * TILE] = tiles[(q & p).bit_count() & 1]


EARLY = {(0, 0), (0, 1)}


def sketch_kernel(
    features, targets, small_ref,
    sketch_hbm, weights_ref,
    feat, targ, upper, coded, factors, flips, mixer,
    out_f, out_k, in_f, in_k, sketch, work, inverse, g_own, g_total, r_own, r_total,
    load_sem, own_sem, store_sem, send_sem, recv_sem, g_send, g_recv, r_send, r_recv, *landing
):
    outer = lax.axis_index("outer")
    me = lax.axis_index("inner")
    x, core = outer // NC, lax.rem(outer, NC)
    y, _ = position(me)

    loads = [
        pltpu.make_async_copy(features, feat, load_sem.at[0]),
        pltpu.make_async_copy(targets, targ, load_sem.at[1]),
    ]
    for load in loads:
        load.start()

    barrier = pltpu.get_barrier_semaphore()

    @pl.loop(1, INNER)
    def _(d):
        pl.semaphore_signal(barrier, inc=1, device_id={"inner": lax.rem(me + d, INNER)}, device_id_type=MESH)

    pl.semaphore_signal(barrier, inc=1, device_id={"outer": x * NC + 1 - core}, device_id_type=MESH)
    for d in range(1, NX):
        pl.semaphore_signal(barrier, inc=1, device_id={"outer": lax.rem(x + d, NX) * NC + core}, device_id_type=MESH)

    order_picks(small_ref, upper, coded, factors)
    fill_signs(small_ref, flips)
    fill_mixer(factors, flips, mixer)
    pl.semaphore_wait(barrier, INNER - 1 + 1 + NX - 1)

    def section(ref, d):
        return ref.at[pl.ds(pl.multiple_of(d * SECTION, SECTION), SECTION)]

    pairs = [(feat, out_f, in_f), (targ, out_k, in_k)]

    def exchange(kind, to, source):
        _, out, into = pairs[kind]
        return pltpu.make_async_remote_copy(
            src_ref=section(out, to),
            dst_ref=section(into, source),
            send_sem=send_sem.at[kind, to],
            recv_sem=recv_sem.at[kind, source],
            device_id={"inner": to},
            device_id_type=MESH,
        )

    span = NZ * SECTION

    def keep(kind, c):
        data, out, _ = pairs[kind]
        at = pl.multiple_of(lax.rem(y + c + 1, NY) * span, span)
        kept = dot(mixer[pl.ds(at, span), :], data[...])
        out[pl.ds(at, span), :] = (kept * (1.0 / 64)).astype(jnp.bfloat16)

    def send(kind, c):
        row = lax.rem(y + c + 1, NY)

        @pl.loop(0, NZ)
        def _(i):
            to = row * NZ + lax.rem(me + i + 1, NZ)

            @pl.when(to != me)
            def _():
                exchange(kind, to, me).start()

    def make(kind):
        loads[kind].wait()
        early = [c for c in range(NY) if (kind, c) in EARLY]
        if early:
            assert early == list(range(len(early)))

            @pl.loop(0, len(early))
            def _(c):
                keep(kind, c)
                send(kind, c)

        @pl.loop(len(early), NY)
        def _(c):
            keep(kind, c)

    def send_rest(kind):
        late = [c for c in range(NY) if (kind, c) not in EARLY]

        @pl.loop(late[0], NY)
        def _(c):
            send(kind, c)

    def arrive(kind):
        own[kind].wait()

        @pl.loop(1, INNER)
        def _(i):
            s = lax.rem(me + i, INNER)
            exchange(kind, s, s).wait()

    def mix(kind):
        first, width = ((0, F), (F, K))[kind]
        into = pairs[kind][2]

        @pl.loop(0, KEEP // 256)
        def _(c):
            at = pl.multiple_of(c * 256, 256)
            mixed = dot(upper[pl.ds(at, 256), :], into[...])
            sketch[pl.ds(at, 256), first : first + width] = (mixed * (1.0 / math.sqrt(INNER))).astype(jnp.bfloat16)

    def eliminate(b, columns):
        at = b * TILE
        pivot = dot(inverse[b], work[at : at + TILE, columns], precision=HIGHEST)
        for first, last in ((0, at), (at + TILE, F)):
            if first < last:
                work[first:last, columns] = work[first:last, columns] - dot(
                    work[first:last, at : at + TILE], pivot, precision=HIGHEST
                )
        work[at : at + TILE, columns] = pivot

    count = len(landing) - len(sum_scratch(R_ROWS, R_FLOWS)[0])
    g = Sum(g_own, g_total, G_ROWS, G_FLOWS, list(landing[:count]), g_send, g_recv)
    r = Sum(r_own, r_total, R_ROWS, R_FLOWS, list(landing[count:]), r_send, r_recv)

    make(0)
    for i in (0, 2):
        rows = dot(out_f[:, i * TILE : (i + 2) * TILE], out_f[:, i * TILE :], TN)
        for n, (p, q) in enumerate(G_BLOCKS):
            if p in (i, i + 1):
                g_own[n * TILE : (n + 1) * TILE, :] = rows[(p - i) * TILE : (p - i + 1) * TILE, (q - i) * TILE : (q - i + 1) * TILE]
    g.step()
    make(1)
    own = [
        pltpu.make_async_copy(section(out_f, me), section(in_f, me), own_sem.at[0]),
        pltpu.make_async_copy(section(out_k, me), section(in_k, me), own_sem.at[1]),
    ]
    for copy in own:
        copy.start()
    g.step()
    for i in (0, 2):
        rows = dot(out_f[:, i * TILE : (i + 2) * TILE], out_k[...], TN)
        for n, (p, q) in enumerate(R_BLOCKS):
            if p in (i, i + 1):
                r_own[n * TILE : (n + 1) * TILE, :] = rows[(p - i) * TILE : (p - i + 1) * TILE, (q - 4) * TILE : (q - 3) * TILE]
    fill_kron(upper)
    r.step()
    g.step()
    r.step()
    g.step()
    r.step()
    g.step()
    r.step()
    send_rest(0)
    send_rest(1)
    g.step()
    g.step()
    r.step()
    g.step()
    assert g.finished

    for n, (i, j) in enumerate(G_BLOCKS):
        tile = g_total[n * TILE : (n + 1) * TILE, :]
        work[i * TILE : (i + 1) * TILE, j * TILE : (j + 1) * TILE] = tile
        if i != j:
            work[j * TILE : (j + 1) * TILE, i * TILE : (i + 1) * TILE] = tile.T
    targets_at = slice(F, F + K)
    for b in range(F // TILE):
        at = b * TILE
        inverse[b] = invert(work[at : at + TILE, at : at + TILE])
        if b < 3:
            eliminate(b, slice(at + TILE, F))
        if b == 0:
            r.step()
        if b == 1:
            r.step()
            r.step()
            assert r.finished
            for n, (i, j) in enumerate(R_BLOCKS):
                work[i * TILE : (i + 1) * TILE, j * TILE : (j + 1) * TILE] = r_total[n * TILE : (n + 1) * TILE, :]
            eliminate(0, targets_at)
        if b:
            eliminate(b, targets_at)
        if b == 2:
            arrive(0)
            mix(0)
    weights_ref[...] = work[:, targets_at]
    arrive(1)
    mix(1)
    store = pltpu.make_async_copy(sketch, sketch_hbm, store_sem)
    store.start()
    store.wait()


def sketch_and_weights(features, targets, small):
    vmem = pl.BlockSpec(memory_space=pltpu.VMEM)
    hbm = pl.BlockSpec(memory_space=pl.ANY)
    f32, bf16 = jnp.float32, jnp.bfloat16
    dma = pltpu.SemaphoreType.DMA
    g_shapes, g_count = sum_scratch(G_ROWS, G_FLOWS)
    r_shapes, r_count = sum_scratch(R_ROWS, R_FLOWS)
    return pl.pallas_call(
        sketch_kernel,
        out_shape=(
            jax.ShapeDtypeStruct((KEEP, F + K), bf16),
            jax.ShapeDtypeStruct((F, K), f32),
        ),
        in_specs=[hbm, hbm, vmem],
        out_specs=(hbm, vmem),
        scratch_shapes=[
            pltpu.VMEM((BLOCK, F), bf16),
            pltpu.VMEM((BLOCK, K), bf16),
            pltpu.VMEM((KEEP, KEEP), bf16),
            pltpu.VMEM((2 * TILE, KEEP), bf16),
            pltpu.VMEM((KEEP, 6 * TILE), bf16),
            pltpu.VMEM((16, BLOCK), bf16),
            pltpu.VMEM((KEEP, BLOCK), bf16),
            pltpu.VMEM((KEEP, F), bf16),
            pltpu.VMEM((KEEP, K), bf16),
            pltpu.VMEM((KEEP, F), bf16),
            pltpu.VMEM((KEEP, K), bf16),
            pltpu.VMEM((KEEP, F + K), bf16),
            pltpu.VMEM((F, F + K), f32),
            pltpu.VMEM((F // TILE, TILE, TILE), f32),
            pltpu.VMEM((G_ROWS, TILE), f32),
            pltpu.VMEM((G_ROWS, TILE), f32),
            pltpu.VMEM((R_ROWS, TILE), f32),
            pltpu.VMEM((R_ROWS, TILE), f32),
            dma((2,)), dma((2,)), dma, dma((2, INNER)), dma((2, INNER)),
            dma((g_count,)), dma((g_count,)), dma((r_count,)), dma((r_count,)),
        ]
        + [pltpu.VMEM(shape, f32) for shape in g_shapes + r_shapes],
        compiler_params=pltpu.CompilerParams(
            collective_id=0, has_side_effects=True, vmem_limit_bytes=51 << 20
        ),
        name="sketch",
    )(features, targets, small)


def predict_kernel(feat, weights_in, sketch_in, sketch_ref, weights_ref, predictions, guess, copy_sem, store_sem):
    copy = pltpu.make_async_copy(sketch_in, sketch_ref, copy_sem)
    copy.start()
    weights_ref[...] = weights_in[...]
    narrow = weights_in[...].astype(jnp.bfloat16)
    chunk = BLOCK // 8
    stores = []
    for c in range(8):
        rows = slice(c * chunk, (c + 1) * chunk)
        guess[rows, :] = dot(feat[rows, :], narrow).astype(jnp.bfloat16)
        where = pl.ds(c * chunk, chunk)
        store = pltpu.make_async_copy(guess.at[where], predictions.at[where], store_sem.at[c])
        store.start()
        stores.append(store)
    for store in stores:
        store.wait()
    copy.wait()


def predict(features, weights, sketch):
    vmem = pl.BlockSpec(memory_space=pltpu.VMEM)
    hbm = pl.BlockSpec(memory_space=pl.ANY)
    return pl.pallas_call(
        predict_kernel,
        out_shape=(
            jax.ShapeDtypeStruct((KEEP, F + K), jnp.bfloat16),
            jax.ShapeDtypeStruct((F, K), jnp.float32),
            jax.ShapeDtypeStruct((BLOCK, K), jnp.bfloat16),
        ),
        in_specs=[vmem, vmem, hbm],
        out_specs=(hbm, vmem, hbm),
        scratch_shapes=[
            pltpu.VMEM((BLOCK, K), jnp.bfloat16),
            pltpu.SemaphoreType.DMA,
            pltpu.SemaphoreType.DMA((8,)),
        ],
        compiler_params=pltpu.CompilerParams(vmem_limit_bytes=12 << 20),
        name="predict",
    )(features, weights, sketch)


def per_device(features, targets, signs, picks, routes):
    sketch, weights = sketch_and_weights(
        features,
        targets,
        jnp.concatenate([signs, picks, routes]).reshape((BLOCK + 2 * KEEP) // TILE, TILE),
    )
    return predict(features, weights, sketch)


def solution(mesh):
    both = ("outer", "inner")
    in_specs = (P(both, None), P(both, None), P(both), P(both), P(both))
    out_specs = (P(both, None), P(), P(both, None))
    return jax.shard_map(per_device, mesh=mesh, in_specs=in_specs, out_specs=out_specs, check_vma=False)
```

```python
import functools
import math

import jax
import jax.numpy as jnp
from jax import lax
from jax.experimental import pallas as pl
from jax.experimental.pallas import tpu as pltpu
from jax.sharding import PartitionSpec as P

F = 512
K = 256
BLOCK = 4096
KEEP = 1024
INNER = 32
NX, NC, NY, NZ = 4, 2, 4, 8
SECTION = KEEP // INNER
TILE = 128
G_BLOCKS = [(i, j) for i in range(4) for j in range(i, 4)]
R_BLOCKS = [(i, j) for i in range(4) for j in range(4, 6)]
G_ROWS = TILE * len(G_BLOCKS)
R_ROWS = TILE * len(R_BLOCKS)
HIGHEST = lax.Precision.HIGHEST
MESH = pl.DeviceIdType.MESH

NN = (((1,), (0,)), ((), ()))
NT = (((1,), (1,)), ((), ()))
TN = (((0,), (0,)), ((), ()))


def dot(a, b, dims=NN, precision=None):
    return lax.dot_general(a, b, dims, precision=precision, preferred_element_type=jnp.float32)


def iota(shape, dim):
    return lax.broadcasted_iota(jnp.int32, shape, dim)


def parity_sign(bits):
    bits = bits ^ (bits >> 4)
    bits = bits ^ (bits >> 2)
    bits = bits ^ (bits >> 1)
    return (1 - 2 * (bits & 1)).astype(jnp.float32)


def position(inner):
    return inner // NZ, lax.rem(inner, NZ)


def order_picks(small_ref, upper_ref, coded_ref, factors_ref):
    first = BLOCK // TILE

    def row_of(first):
        return jnp.concatenate([small_ref[first + i : first + i + 1, :] for i in range(KEEP // TILE)], 1)

    picks = row_of(first)
    routes = row_of(first + KEEP // TILE)

    above = (iota((TILE, TILE), 0) < iota((TILE, TILE), 1)).astype(jnp.float32).astype(jnp.bfloat16)
    for q in range(KEEP // TILE):
        for p in range(KEEP // TILE):
            tile = above if p == q else jnp.full((TILE, TILE), float(p > q), jnp.bfloat16)
            upper_ref[q * TILE : (q + 1) * TILE, p * TILE : (p + 1) * TILE] = tile

    hot = (iota((INNER, KEEP), 0) == routes).astype(jnp.float32)
    before = dot(hot.astype(jnp.bfloat16), upper_ref[...])
    rank = jnp.sum(hot * before, axis=0, keepdims=True)
    place = routes * SECTION + rank.astype(jnp.int32)
    for n, part in enumerate((picks & (TILE - 1), picks >> 7)):
        coded_ref[n * TILE : (n + 1) * TILE, :] = jnp.broadcast_to(
            part.astype(jnp.float32), (TILE, KEEP)
        ).astype(jnp.bfloat16)

    rows = 2 * TILE

    @pl.loop(0, KEEP // rows)
    def _(c):
        at = pl.multiple_of(c * rows, rows)
        chosen = (iota((rows, KEEP), 0) + at == place).astype(jnp.float32).astype(jnp.bfloat16)
        found = dot(chosen, coded_ref[...], NT).astype(jnp.int32)
        low = found[:, :TILE] & iota((rows, TILE), 1)
        factors_ref[pl.ds(at, rows), :TILE] = parity_sign(low).astype(jnp.bfloat16)
        for bit in range(5):
            high = 1 - 2 * ((found[:, TILE:] >> bit) & 1)
            factors_ref[pl.ds(at, rows), (bit + 1) * TILE : (bit + 2) * TILE] = high.astype(jnp.float32).astype(jnp.bfloat16)


def fill_signs(signs_ref, flips_ref):
    for q in range(BLOCK // TILE):
        row = (2 * signs_ref[q : q + 1, :] - 1).astype(jnp.float32)
        flips_ref[:, q * TILE : (q + 1) * TILE] = jnp.broadcast_to(row, (16, TILE)).astype(jnp.bfloat16)


def fill_mixer(factors_ref, flips_ref, mixer_ref):
    rows = 64

    @pl.loop(0, KEEP // rows)
    def _(c):
        at = pl.multiple_of(c * rows, rows)
        here = factors_ref[pl.ds(at, rows), 0:TILE]
        gray = 0
        for step in range(BLOCK // TILE):
            if step:
                bit = (step & -step).bit_length() - 1
                gray ^= 1 << bit
                here = here * factors_ref[pl.ds(at, rows), (bit + 1) * TILE : (bit + 2) * TILE]
            flip = flips_ref[:, gray * TILE : (gray + 1) * TILE]
            flip = jnp.concatenate([flip] * (rows // 16), 0)
            mixer_ref[pl.ds(at, rows), gray * TILE : (gray + 1) * TILE] = here * flip


SIZES = {"core": NC, "plane": NX * NY, "z": NZ}


def flow_scratch(rows, stages):
    shapes, count = [], 0
    for kind, axis in stages:
        n = SIZES[axis]
        count += n - 1
        if kind == "scatter":
            rows //= n
            shapes.append((n - 1, rows, TILE))
        elif kind == "exchange":
            shapes.append((n, rows, TILE))
        else:
            rows *= n
    return shapes, count


class Flow:
    def __init__(self, own, total, first, rows, stages, landing, send, recv):
        self.own, self.total, self.at, self.rows = own, total, first, rows
        self.stages, self.landing, self.send, self.recv = list(stages), list(landing), send, recv
        self.slot = 0
        self.exchanges_left = sum(kind == "exchange" for kind, _ in stages)
        outer = lax.axis_index("outer")
        inner = lax.axis_index("inner")
        self.x, self.y = outer // NC, inner // NZ
        self.place = {"core": lax.rem(outer, NC), "plane": self.x * NY + self.y, "z": lax.rem(inner, NZ)}

    def device(self, axis, to):
        if axis == "core":
            return {"outer": self.x * NC + to}
        if axis == "plane":
            return {"outer": (to // NY) * NC + self.place["core"], "inner": lax.rem(to, NY) * NZ + self.place["z"]}
        return {"inner": self.y * NZ + to}

    def start(self):
        kind, axis = self.stages.pop(0)
        n, me = SIZES[axis], self.place[axis]
        buffer = None if kind == "gather" else self.landing.pop(0)
        copies = []
        for d in range(1, n):
            to = lax.rem(me + d, n)
            if kind == "scatter":
                piece = self.rows // n
                src = self.own.at[pl.ds(pl.multiple_of(self.at + to * piece, 8), piece)]
                dst = buffer.at[d - 1]
            elif kind == "exchange":
                src = self.own.at[pl.ds(pl.multiple_of(self.at, 8), self.rows)]
                dst = buffer.at[me]
            else:
                src = dst = self.total.at[pl.ds(pl.multiple_of(self.at, 8), self.rows)]
            copies.append(
                pltpu.make_async_remote_copy(
                    src_ref=src,
                    dst_ref=dst,
                    send_sem=self.send.at[self.slot],
                    recv_sem=self.recv.at[self.slot],
                    device_id=self.device(axis, to),
                    device_id_type=MESH,
                )
            )
            self.slot += 1
        for copy in copies:
            copy.start()
        self.flight = kind, axis, buffer, copies

    def finish(self):
        kind, axis, buffer, copies = self.flight
        n, me = SIZES[axis], self.place[axis]
        if kind == "exchange":
            buffer[me] = self.own[pl.ds(pl.multiple_of(self.at, 8), self.rows), :]
        for copy in copies:
            copy.wait()
        if kind == "scatter":
            self.rows //= n
            self.at = self.at + me * self.rows
            where = pl.ds(pl.multiple_of(self.at, 8), self.rows)
            terms = [self.own[where, :]] + [buffer[i] for i in range(n - 1)]
        elif kind == "exchange":
            where = pl.ds(pl.multiple_of(self.at, 8), self.rows)
            terms = [buffer[i] for i in range(n)]
        else:
            self.at = self.at - me * self.rows
            self.rows *= n
            return
        while len(terms) > 1:
            terms = [terms[i] + terms[i + 1] for i in range(0, len(terms), 2)]
        self.exchanges_left -= kind == "exchange"
        into = self.own if self.exchanges_left else self.total
        into[where, :] = terms[0]

    def step(self):
        if getattr(self, "flight", None):
            self.finish()
            self.flight = None
        if self.stages:
            self.start()

    def done(self):
        return not self.stages and self.flight is None


CORE = [("scatter", "core")]
PLANE = [("scatter", "plane"), ("exchange", "z"), ("gather", "plane")]
G_FLOWS = [(G_ROWS // NC, PLANE)]
R_FLOWS = [(R_ROWS // NC, PLANE)]


class Sum:
    def __init__(self, own, total, rows, flows, landing, send, recv):
        self.core = Flow(own, total, 0, rows, CORE + [("gather", "core")], landing[:1], send, recv)
        self.core.exchanges_left = 1
        self.flows, self.args = None, (own, total, rows, flows, landing[1:], send, recv)
        self.phase = 0

    def step(self):
        if self.phase == 0:
            self.core.step()
        elif self.phase == 1:
            self.core.finish()
            self.core.flight = None
            own, total, rows, flows, landing, send, recv = self.args
            at, base, self.flows = self.core.at, 2, []
            for size, stages in flows:
                shapes, count = flow_scratch(size, stages)
                used = [landing.pop(0) for _ in shapes]
                flow = Flow(own, total, at, size, stages, used, send, recv)
                flow.slot = base
                base += count
                at = at + size
                flow.step()
                self.flows.append(flow)
        elif not all(flow.done() for flow in self.flows):
            for flow in self.flows:
                if not flow.done():
                    flow.step()
            if all(flow.done() for flow in self.flows):
                self.core.step()
        else:
            self.core.step()
            self.finished = True
        self.phase += 1

    finished = False


def sum_scratch(rows, flows):
    shapes, count = flow_scratch(rows, CORE)
    count += 1
    for size, stages in flows:
        more, n = flow_scratch(size, stages)
        shapes, count = shapes + more, count + n
    return shapes, count


def invert(block):
    lane = iota((8, TILE), 1)
    sub = iota((8, TILE), 0)

    def spread(v, j):
        return jnp.broadcast_to(v[:, j : j + 1], (8, TILE))

    def down(v, i):
        return jnp.broadcast_to(v[i : i + 1, :], (8, TILE))

    v = [block[8 * i : 8 * i + 8, :] for i in range(16)]
    for g in range(16):
        base = 8 * g
        now = v[g]
        cols = [spread(now, base + j) for j in range(8)]
        for s in range(8):
            over = 1.0 / down(cols[s], s)
            mult = jnp.where(sub == s, 0.0, cols[s])
            row = jnp.where(lane == base + s, 1.0, down(now, s)) * over
            now = jnp.where(sub == s, row, jnp.where(lane == base + s, 0.0, now) - mult * row)
            for j in range(s + 1, 8):
                pivot = down(cols[j], s) * over
                cols[j] = jnp.where(sub == s, pivot, cols[j] - mult * pivot)
        rows = [down(now, j) for j in range(8)]
        panel = (lane >= base) & (lane < base + 8)
        new = []
        for i in range(16):
            if i == g:
                new.append(now)
                continue
            p = [spread(v[i], base + j) * rows[j] for j in range(8)]
            p = ((p[0] + p[1]) + (p[2] + p[3])) + ((p[4] + p[5]) + (p[6] + p[7]))
            new.append(jnp.where(panel, 0.0, v[i]) - p)
        v = new
    return jnp.concatenate(v, 0)


def fill_kron(kron):
    a, b = iota((TILE, TILE), 0), iota((TILE, TILE), 1)
    sign = parity_sign((a // SECTION) & (b // SECTION))
    tile = jnp.where((a ^ b) & (SECTION - 1) == 0, sign, 0.0)
    tiles = [tile.astype(jnp.bfloat16), (-tile).astype(jnp.bfloat16)]
    for q in range(KEEP // TILE):
        for p in range(KEEP // TILE):
            kron[q * TILE : (q + 1) * TILE, p * TILE : (p + 1) * TILE] = tiles[(q & p).bit_count() & 1]


EARLY = {(0, 0), (0, 1)}


def sketch_kernel(
    features, targets, small_ref,
    sketch_hbm, weights_ref,
    feat, targ, upper, coded, factors, flips, mixer,
    out_f, out_k, in_f, in_k, sketch, work, inverse, g_own, g_total, r_own, r_total,
    load_sem, own_sem, store_sem, send_sem, recv_sem, g_send, g_recv, r_send, r_recv, *landing
):
    outer = lax.axis_index("outer")
    me = lax.axis_index("inner")
    x, core = outer // NC, lax.rem(outer, NC)
    y, z = position(me)

    loads = [
        pltpu.make_async_copy(features, feat, load_sem.at[0]),
        pltpu.make_async_copy(targets, targ, load_sem.at[1]),
    ]
    for load in loads:
        load.start()

    barrier = pltpu.get_barrier_semaphore()

    @pl.loop(1, INNER)
    def _(d):
        pl.semaphore_signal(barrier, inc=1, device_id={"inner": lax.rem(me + d, INNER)}, device_id_type=MESH)

    pl.semaphore_signal(barrier, inc=1, device_id={"outer": x * NC + 1 - core}, device_id_type=MESH)

    @pl.loop(1, NX)
    def _(d):
        @pl.loop(0, NY)
        def _(row):
            pl.semaphore_signal(
                barrier,
                inc=1,
                device_id={"outer": lax.rem(x + d, NX) * NC + core, "inner": row * NZ + z},
                device_id_type=MESH,
            )

    order_picks(small_ref, upper, coded, factors)
    fill_signs(small_ref, flips)
    fill_mixer(factors, flips, mixer)
    pl.semaphore_wait(barrier, INNER - 1 + 1 + (NX - 1) * NY)

    def section(ref, d):
        return ref.at[pl.ds(pl.multiple_of(d * SECTION, SECTION), SECTION)]

    pairs = [(feat, out_f, in_f), (targ, out_k, in_k)]

    def exchange(kind, to, source):
        _, out, into = pairs[kind]
        return pltpu.make_async_remote_copy(
            src_ref=section(out, to),
            dst_ref=section(into, source),
            send_sem=send_sem.at[kind, to],
            recv_sem=recv_sem.at[kind, source],
            device_id={"inner": to},
            device_id_type=MESH,
        )

    span = NZ * SECTION

    def keep(kind, c):
        data, out, _ = pairs[kind]
        at = pl.multiple_of(lax.rem(y + c + 1, NY) * span, span)
        kept = dot(mixer[pl.ds(at, span), :], data[...])
        out[pl.ds(at, span), :] = (kept * (1.0 / 64)).astype(jnp.bfloat16)

    def send(kind, c):
        row = lax.rem(y + c + 1, NY)

        @pl.loop(0, NZ)
        def _(i):
            to = row * NZ + lax.rem(me + i + 1, NZ)

            @pl.when(to != me)
            def _():
                exchange(kind, to, me).start()

    def make(kind):
        loads[kind].wait()
        early = [c for c in range(NY) if (kind, c) in EARLY]
        if early:
            assert early == list(range(len(early)))

            @pl.loop(0, len(early))
            def _(c):
                keep(kind, c)
                send(kind, c)

        @pl.loop(len(early), NY)
        def _(c):
            keep(kind, c)

    def send_rest(kind):
        late = [c for c in range(NY) if (kind, c) not in EARLY]

        @pl.loop(late[0], NY)
        def _(c):
            send(kind, c)

    def arrive(kind):
        own[kind].wait()

        @pl.loop(1, INNER)
        def _(i):
            s = lax.rem(me + i, INNER)
            exchange(kind, s, s).wait()

    def mix(kind):
        first, width = ((0, F), (F, K))[kind]
        into = pairs[kind][2]

        @pl.loop(0, KEEP // 256)
        def _(c):
            at = pl.multiple_of(c * 256, 256)
            mixed = dot(upper[pl.ds(at, 256), :], into[...])
            sketch[pl.ds(at, 256), first : first + width] = (mixed * (1.0 / math.sqrt(INNER))).astype(jnp.bfloat16)

    def eliminate(b, columns):
        at = b * TILE
        pivot = dot(inverse[b], work[at : at + TILE, columns], precision=HIGHEST)
        for first, last in ((0, at), (at + TILE, F)):
            if first < last:
                work[first:last, columns] = work[first:last, columns] - dot(
                    work[first:last, at : at + TILE], pivot, precision=HIGHEST
                )
        work[at : at + TILE, columns] = pivot

    count = len(landing) - len(sum_scratch(R_ROWS, R_FLOWS)[0])
    g = Sum(g_own, g_total, G_ROWS, G_FLOWS, list(landing[:count]), g_send, g_recv)
    r = Sum(r_own, r_total, R_ROWS, R_FLOWS, list(landing[count:]), r_send, r_recv)

    make(0)
    for i in (0, 2):
        rows = dot(out_f[:, i * TILE : (i + 2) * TILE], out_f[:, i * TILE :], TN)
        for n, (p, q) in enumerate(G_BLOCKS):
            if p in (i, i + 1):
                g_own[n * TILE : (n + 1) * TILE, :] = rows[(p - i) * TILE : (p - i + 1) * TILE, (q - i) * TILE : (q - i + 1) * TILE]
    g.step()
    fill_kron(upper)
    g.step()
    make(1)
    own = [
        pltpu.make_async_copy(section(out_f, me), section(in_f, me), own_sem.at[0]),
        pltpu.make_async_copy(section(out_k, me), section(in_k, me), own_sem.at[1]),
    ]
    for copy in own:
        copy.start()
    for i in (0, 2):
        rows = dot(out_f[:, i * TILE : (i + 2) * TILE], out_k[...], TN)
        for n, (p, q) in enumerate(R_BLOCKS):
            if p in (i, i + 1):
                r_own[n * TILE : (n + 1) * TILE, :] = rows[(p - i) * TILE : (p - i + 1) * TILE, (q - 4) * TILE : (q - 3) * TILE]
    r.step()
    g.step()
    r.step()
    g.step()
    r.step()
    send_rest(0)
    send_rest(1)
    g.step()
    r.step()

    def unpack(half):
        for n in range(half * len(G_BLOCKS) // 2, (half + 1) * len(G_BLOCKS) // 2):
            i, j = G_BLOCKS[n]
            tile = g_total[n * TILE : (n + 1) * TILE, :]
            work[i * TILE : (i + 1) * TILE, j * TILE : (j + 1) * TILE] = tile
            if i != j:
                work[j * TILE : (j + 1) * TILE, i * TILE : (i + 1) * TILE] = tile.T

    pl.when(core == 0)(functools.partial(unpack, 0))
    pl.when(core == 1)(functools.partial(unpack, 1))
    g.step()
    assert g.finished
    pl.when(core == 0)(functools.partial(unpack, 1))
    pl.when(core == 1)(functools.partial(unpack, 0))
    targets_at = slice(F, F + K)
    for b in range(F // TILE):
        at = b * TILE
        inverse[b] = invert(work[at : at + TILE, at : at + TILE])
        if b < 3:
            eliminate(b, slice(at + TILE, F))
        if b == 0:
            r.step()
        if b == 1:
            r.step()
            assert r.finished
            for n, (i, j) in enumerate(R_BLOCKS):
                work[i * TILE : (i + 1) * TILE, j * TILE : (j + 1) * TILE] = r_total[n * TILE : (n + 1) * TILE, :]
            eliminate(0, targets_at)
        if b:
            eliminate(b, targets_at)
        if b == 2:
            arrive(0)
            mix(0)
    weights_ref[...] = work[:, targets_at]
    arrive(1)
    mix(1)
    store = pltpu.make_async_copy(sketch, sketch_hbm, store_sem)
    store.start()
    store.wait()


def sketch_and_weights(features, targets, small):
    vmem = pl.BlockSpec(memory_space=pltpu.VMEM)
    hbm = pl.BlockSpec(memory_space=pl.ANY)
    f32, bf16 = jnp.float32, jnp.bfloat16
    dma = pltpu.SemaphoreType.DMA
    g_shapes, g_count = sum_scratch(G_ROWS, G_FLOWS)
    r_shapes, r_count = sum_scratch(R_ROWS, R_FLOWS)
    return pl.pallas_call(
        sketch_kernel,
        out_shape=(
            jax.ShapeDtypeStruct((KEEP, F + K), bf16),
            jax.ShapeDtypeStruct((F, K), f32),
        ),
        in_specs=[hbm, hbm, vmem],
        out_specs=(hbm, vmem),
        scratch_shapes=[
            pltpu.VMEM((BLOCK, F), bf16),
            pltpu.VMEM((BLOCK, K), bf16),
            pltpu.VMEM((KEEP, KEEP), bf16),
            pltpu.VMEM((2 * TILE, KEEP), bf16),
            pltpu.VMEM((KEEP, 6 * TILE), bf16),
            pltpu.VMEM((16, BLOCK), bf16),
            pltpu.VMEM((KEEP, BLOCK), bf16),
            pltpu.VMEM((KEEP, F), bf16),
            pltpu.VMEM((KEEP, K), bf16),
            pltpu.VMEM((KEEP, F), bf16),
            pltpu.VMEM((KEEP, K), bf16),
            pltpu.VMEM((KEEP, F + K), bf16),
            pltpu.VMEM((F, F + K), f32),
            pltpu.VMEM((F // TILE, TILE, TILE), f32),
            pltpu.VMEM((G_ROWS, TILE), f32),
            pltpu.VMEM((G_ROWS, TILE), f32),
            pltpu.VMEM((R_ROWS, TILE), f32),
            pltpu.VMEM((R_ROWS, TILE), f32),
            dma((2,)), dma((2,)), dma, dma((2, INNER)), dma((2, INNER)),
            dma((g_count,)), dma((g_count,)), dma((r_count,)), dma((r_count,)),
        ]
        + [pltpu.VMEM(shape, f32) for shape in g_shapes + r_shapes],
        compiler_params=pltpu.CompilerParams(
            collective_id=0, has_side_effects=True, vmem_limit_bytes=51 << 20
        ),
        name="sketch",
    )(features, targets, small)


def predict_kernel(feat, weights_in, sketch_in, sketch_ref, weights_ref, predictions, guess, copy_sem, store_sem):
    copy = pltpu.make_async_copy(sketch_in, sketch_ref, copy_sem)
    copy.start()
    weights_ref[...] = weights_in[...]
    narrow = weights_in[...].astype(jnp.bfloat16)
    chunk = BLOCK // 8
    stores = []
    for c in range(8):
        rows = slice(c * chunk, (c + 1) * chunk)
        guess[rows, :] = dot(feat[rows, :], narrow).astype(jnp.bfloat16)
        where = pl.ds(c * chunk, chunk)
        store = pltpu.make_async_copy(guess.at[where], predictions.at[where], store_sem.at[c])
        store.start()
        stores.append(store)
    for store in stores:
        store.wait()
    copy.wait()


def predict(features, weights, sketch):
    vmem = pl.BlockSpec(memory_space=pltpu.VMEM)
    hbm = pl.BlockSpec(memory_space=pl.ANY)
    return pl.pallas_call(
        predict_kernel,
        out_shape=(
            jax.ShapeDtypeStruct((KEEP, F + K), jnp.bfloat16),
            jax.ShapeDtypeStruct((F, K), jnp.float32),
            jax.ShapeDtypeStruct((BLOCK, K), jnp.bfloat16),
        ),
        in_specs=[vmem, vmem, hbm],
        out_specs=(hbm, vmem, hbm),
        scratch_shapes=[
            pltpu.VMEM((BLOCK, K), jnp.bfloat16),
            pltpu.SemaphoreType.DMA,
            pltpu.SemaphoreType.DMA((8,)),
        ],
        compiler_params=pltpu.CompilerParams(vmem_limit_bytes=12 << 20),
        name="predict",
    )(features, weights, sketch)


def per_device(features, targets, signs, picks, routes):
    sketch, weights = sketch_and_weights(
        features,
        targets,
        jnp.concatenate([signs, picks, routes]).reshape((BLOCK + 2 * KEEP) // TILE, TILE),
    )
    return predict(features, weights, sketch)


def solution(mesh):
    both = ("outer", "inner")
    in_specs = (P(both, None), P(both, None), P(both), P(both), P(both))
    out_specs = (P(both, None), P(), P(both, None))
    return jax.shard_map(per_device, mesh=mesh, in_specs=in_specs, out_specs=out_specs, check_vma=False)
```

```python
import functools
import math

import jax
import jax.numpy as jnp
from jax import lax
from jax.experimental import pallas as pl
from jax.experimental.pallas import tpu as pltpu
from jax.sharding import PartitionSpec as P

F = 512
K = 256
BLOCK = 4096
KEEP = 1024
INNER = 32
NX, NC, NY, NZ = 4, 2, 4, 8
SECTION = KEEP // INNER
TILE = 128
G_BLOCKS = [(i, j) for i in range(4) for j in range(i, 4)]
R_BLOCKS = [(i, j) for i in range(4) for j in range(4, 6)]
G_ROWS = TILE * len(G_BLOCKS)
R_ROWS = TILE * len(R_BLOCKS)
MESH = pl.DeviceIdType.MESH

NN = (((1,), (0,)), ((), ()))
NT = (((1,), (1,)), ((), ()))
TN = (((0,), (0,)), ((), ()))


def dot(a, b, dims=NN, precision=None):
    return lax.dot_general(a, b, dims, precision=precision, preferred_element_type=jnp.float32)


def iota(shape, dim):
    return lax.broadcasted_iota(jnp.int32, shape, dim)


def parity_sign(bits):
    bits = bits ^ (bits >> 4)
    bits = bits ^ (bits >> 2)
    bits = bits ^ (bits >> 1)
    return (1 - 2 * (bits & 1)).astype(jnp.float32)


def position(inner):
    return inner // NZ, lax.rem(inner, NZ)


def order_picks(small_ref, upper_ref, coded_ref, factors_ref):
    first = BLOCK // TILE

    def row_of(first):
        return jnp.concatenate([small_ref[first + i : first + i + 1, :] for i in range(KEEP // TILE)], 1)

    picks = row_of(first)
    routes = row_of(first + KEEP // TILE)

    above = (iota((TILE, TILE), 0) < iota((TILE, TILE), 1)).astype(jnp.float32).astype(jnp.bfloat16)
    for q in range(KEEP // TILE):
        for p in range(KEEP // TILE):
            tile = above if p == q else jnp.full((TILE, TILE), float(p > q), jnp.bfloat16)
            upper_ref[q * TILE : (q + 1) * TILE, p * TILE : (p + 1) * TILE] = tile

    hot = (iota((INNER, KEEP), 0) == routes).astype(jnp.float32)
    before = dot(hot.astype(jnp.bfloat16), upper_ref[...])
    rank = jnp.sum(hot * before, axis=0, keepdims=True)
    place = routes * SECTION + rank.astype(jnp.int32)
    for n, part in enumerate((picks & (TILE - 1), picks >> 7)):
        coded_ref[n * TILE : (n + 1) * TILE, :] = jnp.broadcast_to(
            part.astype(jnp.float32), (TILE, KEEP)
        ).astype(jnp.bfloat16)

    rows = 2 * TILE

    @pl.loop(0, KEEP // rows)
    def _(c):
        at = pl.multiple_of(c * rows, rows)
        chosen = (iota((rows, KEEP), 0) + at == place).astype(jnp.float32).astype(jnp.bfloat16)
        found = dot(chosen, coded_ref[...], NT).astype(jnp.int32)
        low = found[:, :TILE] & iota((rows, TILE), 1)
        factors_ref[pl.ds(at, rows), :TILE] = parity_sign(low).astype(jnp.bfloat16)
        for bit in range(5):
            high = 1 - 2 * ((found[:, TILE:] >> bit) & 1)
            factors_ref[pl.ds(at, rows), (bit + 1) * TILE : (bit + 2) * TILE] = high.astype(jnp.float32).astype(jnp.bfloat16)


def fill_signs(signs_ref, flips_ref):
    for q in range(BLOCK // TILE):
        row = (2 * signs_ref[q : q + 1, :] - 1).astype(jnp.float32)
        flips_ref[:, q * TILE : (q + 1) * TILE] = jnp.broadcast_to(row, (16, TILE)).astype(jnp.bfloat16)


def fill_mixer(factors_ref, flips_ref, mixer_ref):
    rows = 64

    @pl.loop(0, KEEP // rows)
    def _(c):
        at = pl.multiple_of(c * rows, rows)
        here = factors_ref[pl.ds(at, rows), 0:TILE]
        gray = 0
        for step in range(BLOCK // TILE):
            if step:
                bit = (step & -step).bit_length() - 1
                gray ^= 1 << bit
                here = here * factors_ref[pl.ds(at, rows), (bit + 1) * TILE : (bit + 2) * TILE]
            flip = flips_ref[:, gray * TILE : (gray + 1) * TILE]
            flip = jnp.concatenate([flip] * (rows // 16), 0)
            mixer_ref[pl.ds(at, rows), gray * TILE : (gray + 1) * TILE] = here * flip


SIZES = {"core": NC, "plane": NX * NY, "z": NZ}


def flow_scratch(rows, stages):
    shapes, count = [], 0
    for kind, axis in stages:
        n = SIZES[axis]
        count += n - 1
        if kind == "scatter":
            rows //= n
            shapes.append((n - 1, rows, TILE))
        elif kind == "exchange":
            shapes.append((n, rows, TILE))
        else:
            rows *= n
    return shapes, count


class Flow:
    def __init__(self, own, total, first, rows, stages, landing, send, recv):
        self.own, self.total, self.at, self.rows = own, total, first, rows
        self.stages, self.landing, self.send, self.recv = list(stages), list(landing), send, recv
        self.slot = 0
        self.exchanges_left = sum(kind == "exchange" for kind, _ in stages)
        outer = lax.axis_index("outer")
        inner = lax.axis_index("inner")
        self.x, self.y = outer // NC, inner // NZ
        self.place = {"core": lax.rem(outer, NC), "plane": self.x * NY + self.y, "z": lax.rem(inner, NZ)}

    def device(self, axis, to):
        if axis == "core":
            return {"outer": self.x * NC + to}
        if axis == "plane":
            return {"outer": (to // NY) * NC + self.place["core"], "inner": lax.rem(to, NY) * NZ + self.place["z"]}
        return {"inner": self.y * NZ + to}

    def start(self):
        kind, axis = self.stages.pop(0)
        n, me = SIZES[axis], self.place[axis]
        buffer = None if kind == "gather" else self.landing.pop(0)
        copies = []
        for d in range(1, n):
            to = lax.rem(me + d, n)
            if kind == "scatter":
                piece = self.rows // n
                src = self.own.at[pl.ds(pl.multiple_of(self.at + to * piece, 8), piece)]
                dst = buffer.at[d - 1]
            elif kind == "exchange":
                src = self.own.at[pl.ds(pl.multiple_of(self.at, 8), self.rows)]
                dst = buffer.at[me]
            else:
                src = dst = self.total.at[pl.ds(pl.multiple_of(self.at, 8), self.rows)]
            copies.append(
                pltpu.make_async_remote_copy(
                    src_ref=src,
                    dst_ref=dst,
                    send_sem=self.send.at[self.slot],
                    recv_sem=self.recv.at[self.slot],
                    device_id=self.device(axis, to),
                    device_id_type=MESH,
                )
            )
            self.slot += 1
        for copy in copies:
            copy.start()
        self.flight = kind, axis, buffer, copies

    def finish(self):
        kind, axis, buffer, copies = self.flight
        n, me = SIZES[axis], self.place[axis]
        if kind == "exchange":
            buffer[me] = self.own[pl.ds(pl.multiple_of(self.at, 8), self.rows), :]
        for copy in copies:
            copy.wait()
        if kind == "scatter":
            self.rows //= n
            self.at = self.at + me * self.rows
            where = pl.ds(pl.multiple_of(self.at, 8), self.rows)
            terms = [self.own[where, :]] + [buffer[i] for i in range(n - 1)]
        elif kind == "exchange":
            where = pl.ds(pl.multiple_of(self.at, 8), self.rows)
            terms = [buffer[i] for i in range(n)]
        else:
            self.at = self.at - me * self.rows
            self.rows *= n
            return
        while len(terms) > 1:
            terms = [terms[i] + terms[i + 1] for i in range(0, len(terms), 2)]
        self.exchanges_left -= kind == "exchange"
        into = self.own if self.exchanges_left else self.total
        into[where, :] = terms[0]

    def step(self):
        if getattr(self, "flight", None):
            self.finish()
            self.flight = None
        if self.stages:
            self.start()

    def done(self):
        return not self.stages and self.flight is None


CORE = [("scatter", "core")]
PLANE = [("scatter", "plane"), ("exchange", "z"), ("gather", "plane")]
G_FLOWS = [(G_ROWS // NC, PLANE)]
R_FLOWS = [(R_ROWS // NC, PLANE)]


class Sum:
    def __init__(self, own, total, rows, flows, landing, send, recv):
        self.core = Flow(own, total, 0, rows, CORE + [("gather", "core")], landing[:1], send, recv)
        self.core.exchanges_left = 1
        self.flows, self.args = None, (own, total, rows, flows, landing[1:], send, recv)
        self.phase = 0

    def step(self):
        if self.phase == 0:
            self.core.step()
        elif self.phase == 1:
            self.core.finish()
            self.core.flight = None
            own, total, rows, flows, landing, send, recv = self.args
            at, base, self.flows = self.core.at, 2, []
            for size, stages in flows:
                shapes, count = flow_scratch(size, stages)
                used = [landing.pop(0) for _ in shapes]
                flow = Flow(own, total, at, size, stages, used, send, recv)
                flow.slot = base
                base += count
                at = at + size
                flow.step()
                self.flows.append(flow)
        elif not all(flow.done() for flow in self.flows):
            for flow in self.flows:
                if not flow.done():
                    flow.step()
            if all(flow.done() for flow in self.flows):
                self.core.step()
        else:
            self.core.step()
            self.finished = True
        self.phase += 1

    finished = False


def sum_scratch(rows, flows):
    shapes, count = flow_scratch(rows, CORE)
    count += 1
    for size, stages in flows:
        more, n = flow_scratch(size, stages)
        shapes, count = shapes + more, count + n
    return shapes, count


def thirds(a):
    high = a.astype(jnp.bfloat16)
    rest = a - high.astype(jnp.float32)
    middle = rest.astype(jnp.bfloat16)
    return high, middle, (rest - middle.astype(jnp.float32)).astype(jnp.bfloat16)


def dot_exact(a, b):
    ah, am, al = thirds(a)
    bh, bm, bl = thirds(b)
    return dot(jnp.concatenate([ah, ah, am, am, ah, al], 1), jnp.concatenate([bh, bm, bh, bm, bl, bh], 0))


def invert(block):
    lane = iota((8, TILE), 1)
    sub = iota((8, TILE), 0)

    def spread(v, j):
        return jnp.broadcast_to(v[:, j : j + 1], (8, TILE))

    def down(v, i):
        return jnp.broadcast_to(v[i : i + 1, :], (8, TILE))

    v = [block[8 * i : 8 * i + 8, :] for i in range(16)]
    for g in range(16):
        base = 8 * g
        now = v[g]
        cols = [spread(now, base + j) for j in range(8)]
        for s in range(8):
            over = 1.0 / down(cols[s], s)
            mult = jnp.where(sub == s, 0.0, cols[s])
            for j in range(s + 1, 8):
                pivot = down(cols[j], s) * over
                cols[j] = jnp.where(sub == s, pivot, cols[j] - mult * pivot)
            row = jnp.where(lane == base + s, 1.0, down(now, s)) * over
            now = jnp.where(sub == s, row, jnp.where(lane == base + s, 0.0, now) - mult * row)
        rows = [down(now, j) for j in range(8)]
        panel = (lane >= base) & (lane < base + 8)
        new = []
        for i in range(16):
            if i == g:
                new.append(now)
                continue
            p = [spread(v[i], base + j) * rows[j] for j in range(8)]
            p = ((p[0] + p[1]) + (p[2] + p[3])) + ((p[4] + p[5]) + (p[6] + p[7]))
            new.append(jnp.where(panel, 0.0, v[i]) - p)
        v = new
    return jnp.concatenate(v, 0)


def fill_kron(kron):
    a, b = iota((TILE, TILE), 0), iota((TILE, TILE), 1)
    sign = parity_sign((a // SECTION) & (b // SECTION))
    tile = jnp.where((a ^ b) & (SECTION - 1) == 0, sign, 0.0)
    tiles = [tile.astype(jnp.bfloat16), (-tile).astype(jnp.bfloat16)]
    for q in range(KEEP // TILE):
        for p in range(KEEP // TILE):
            kron[q * TILE : (q + 1) * TILE, p * TILE : (p + 1) * TILE] = tiles[(q & p).bit_count() & 1]


EARLY = {(0, 0)}


def sketch_kernel(
    features, targets, small_ref,
    sketch_hbm, weights_ref,
    feat, targ, upper, coded, factors, flips, mixer,
    out_f, out_k, in_f, in_k, sketch, work, inverse, g_own, g_total, r_own, r_total,
    load_sem, own_sem, store_sem, send_sem, recv_sem, g_send, g_recv, r_send, r_recv, *landing
):
    outer = lax.axis_index("outer")
    me = lax.axis_index("inner")
    x, core = outer // NC, lax.rem(outer, NC)
    y, z = position(me)

    loads = [
        pltpu.make_async_copy(features, feat, load_sem.at[0]),
        pltpu.make_async_copy(targets, targ, load_sem.at[1]),
    ]
    for load in loads:
        load.start()

    barrier = pltpu.get_barrier_semaphore()

    @pl.loop(1, INNER)
    def _(d):
        pl.semaphore_signal(barrier, inc=1, device_id={"inner": lax.rem(me + d, INNER)}, device_id_type=MESH)

    pl.semaphore_signal(barrier, inc=1, device_id={"outer": x * NC + 1 - core}, device_id_type=MESH)

    @pl.loop(1, NX)
    def _(d):
        @pl.loop(0, NY)
        def _(row):
            pl.semaphore_signal(
                barrier,
                inc=1,
                device_id={"outer": lax.rem(x + d, NX) * NC + core, "inner": row * NZ + z},
                device_id_type=MESH,
            )

    order_picks(small_ref, upper, coded, factors)
    fill_signs(small_ref, flips)
    fill_mixer(factors, flips, mixer)
    pl.semaphore_wait(barrier, INNER - 1 + 1 + (NX - 1) * NY)

    def section(ref, d):
        return ref.at[pl.ds(pl.multiple_of(d * SECTION, SECTION), SECTION)]

    pairs = [(feat, out_f, in_f), (targ, out_k, in_k)]

    def exchange(kind, to, source):
        _, out, into = pairs[kind]
        return pltpu.make_async_remote_copy(
            src_ref=section(out, to),
            dst_ref=section(into, source),
            send_sem=send_sem.at[kind, to],
            recv_sem=recv_sem.at[kind, source],
            device_id={"inner": to},
            device_id_type=MESH,
        )

    span = NZ * SECTION

    def keep(kind, c):
        data, out, _ = pairs[kind]
        at = pl.multiple_of(lax.rem(y + c + 1, NY) * span, span)
        kept = dot(mixer[pl.ds(at, span), :], data[...])
        out[pl.ds(at, span), :] = (kept * (1.0 / 64)).astype(jnp.bfloat16)

    def send(kind, c):
        row = lax.rem(y + c + 1, NY)

        @pl.loop(0, NZ)
        def _(i):
            to = row * NZ + lax.rem(me + i + 1, NZ)

            @pl.when(to != me)
            def _():
                exchange(kind, to, me).start()

    def make(kind):
        loads[kind].wait()
        early = [c for c in range(NY) if (kind, c) in EARLY]
        if early:
            assert early == list(range(len(early)))

            @pl.loop(0, len(early))
            def _(c):
                keep(kind, c)
                send(kind, c)

        @pl.loop(len(early), NY)
        def _(c):
            keep(kind, c)

    def send_rest(kind):
        late = [c for c in range(NY) if (kind, c) not in EARLY]

        @pl.loop(late[0], NY)
        def _(c):
            send(kind, c)

    def arrive(kind):
        own[kind].wait()

        @pl.loop(1, INNER)
        def _(i):
            s = lax.rem(me + i, INNER)
            exchange(kind, s, s).wait()

    def mix(kind):
        first, width = ((0, F), (F, K))[kind]
        into = pairs[kind][2]

        @pl.loop(0, KEEP // 256)
        def _(c):
            at = pl.multiple_of(c * 256, 256)
            mixed = dot(upper[pl.ds(at, 256), :], into[...])
            sketch[pl.ds(at, 256), first : first + width] = (mixed * (1.0 / math.sqrt(INNER))).astype(jnp.bfloat16)

    def eliminate(b, columns):
        at = b * TILE
        pivot = dot_exact(inverse[b], work[at : at + TILE, columns])
        for first, last in ((0, at), (at + TILE, F)):
            if first < last:
                work[first:last, columns] = work[first:last, columns] - dot_exact(
                    work[first:last, at : at + TILE], pivot
                )
        work[at : at + TILE, columns] = pivot

    count = len(landing) - len(sum_scratch(R_ROWS, R_FLOWS)[0])
    g = Sum(g_own, g_total, G_ROWS, G_FLOWS, list(landing[:count]), g_send, g_recv)
    r = Sum(r_own, r_total, R_ROWS, R_FLOWS, list(landing[count:]), r_send, r_recv)

    make(0)
    for i in (0, 2):
        rows = dot(out_f[:, i * TILE : (i + 2) * TILE], out_f[:, i * TILE :], TN)
        for n, (p, q) in enumerate(G_BLOCKS):
            if p in (i, i + 1):
                g_own[n * TILE : (n + 1) * TILE, :] = rows[(p - i) * TILE : (p - i + 1) * TILE, (q - i) * TILE : (q - i + 1) * TILE]
    g.step()
    fill_kron(upper)
    g.step()
    make(1)
    own = [
        pltpu.make_async_copy(section(out_f, me), section(in_f, me), own_sem.at[0]),
        pltpu.make_async_copy(section(out_k, me), section(in_k, me), own_sem.at[1]),
    ]
    for copy in own:
        copy.start()
    for i in (0, 2):
        rows = dot(out_f[:, i * TILE : (i + 2) * TILE], out_k[...], TN)
        for n, (p, q) in enumerate(R_BLOCKS):
            if p in (i, i + 1):
                r_own[n * TILE : (n + 1) * TILE, :] = rows[(p - i) * TILE : (p - i + 1) * TILE, (q - 4) * TILE : (q - 3) * TILE]
    r.step()
    g.step()
    r.step()
    g.step()
    r.step()
    send_rest(0)
    send_rest(1)
    g.step()
    r.step()

    def unpack(half):
        for n in range(half * len(G_BLOCKS) // 2, (half + 1) * len(G_BLOCKS) // 2):
            i, j = G_BLOCKS[n]
            tile = g_total[n * TILE : (n + 1) * TILE, :]
            work[i * TILE : (i + 1) * TILE, j * TILE : (j + 1) * TILE] = tile
            if i != j:
                work[j * TILE : (j + 1) * TILE, i * TILE : (i + 1) * TILE] = tile.T

    pl.when(core == 0)(functools.partial(unpack, 0))
    pl.when(core == 1)(functools.partial(unpack, 1))
    g.step()
    assert g.finished
    pl.when(core == 0)(functools.partial(unpack, 1))
    pl.when(core == 1)(functools.partial(unpack, 0))
    targets_at = slice(F, F + K)
    for b in range(F // TILE):
        at = b * TILE
        inverse[b] = invert(work[at : at + TILE, at : at + TILE])
        if b < 3:
            eliminate(b, slice(at + TILE, F))
        if b == 0:
            r.step()
        if b == 1:
            r.step()
            assert r.finished
            for n, (i, j) in enumerate(R_BLOCKS):
                work[i * TILE : (i + 1) * TILE, j * TILE : (j + 1) * TILE] = r_total[n * TILE : (n + 1) * TILE, :]
            eliminate(0, targets_at)
        if b:
            eliminate(b, targets_at)
        if b == 2:
            arrive(0)
            mix(0)
    weights_ref[...] = work[:, targets_at]
    arrive(1)
    mix(1)
    store = pltpu.make_async_copy(sketch, sketch_hbm, store_sem)
    store.start()
    store.wait()


def sketch_and_weights(features, targets, small):
    vmem = pl.BlockSpec(memory_space=pltpu.VMEM)
    hbm = pl.BlockSpec(memory_space=pl.ANY)
    f32, bf16 = jnp.float32, jnp.bfloat16
    dma = pltpu.SemaphoreType.DMA
    g_shapes, g_count = sum_scratch(G_ROWS, G_FLOWS)
    r_shapes, r_count = sum_scratch(R_ROWS, R_FLOWS)
    return pl.pallas_call(
        sketch_kernel,
        out_shape=(
            jax.ShapeDtypeStruct((KEEP, F + K), bf16),
            jax.ShapeDtypeStruct((F, K), f32),
        ),
        in_specs=[hbm, hbm, vmem],
        out_specs=(hbm, vmem),
        scratch_shapes=[
            pltpu.VMEM((BLOCK, F), bf16),
            pltpu.VMEM((BLOCK, K), bf16),
            pltpu.VMEM((KEEP, KEEP), bf16),
            pltpu.VMEM((2 * TILE, KEEP), bf16),
            pltpu.VMEM((KEEP, 6 * TILE), bf16),
            pltpu.VMEM((16, BLOCK), bf16),
            pltpu.VMEM((KEEP, BLOCK), bf16),
            pltpu.VMEM((KEEP, F), bf16),
            pltpu.VMEM((KEEP, K), bf16),
            pltpu.VMEM((KEEP, F), bf16),
            pltpu.VMEM((KEEP, K), bf16),
            pltpu.VMEM((KEEP, F + K), bf16),
            pltpu.VMEM((F, F + K), f32),
            pltpu.VMEM((F // TILE, TILE, TILE), f32),
            pltpu.VMEM((G_ROWS, TILE), f32),
            pltpu.VMEM((G_ROWS, TILE), f32),
            pltpu.VMEM((R_ROWS, TILE), f32),
            pltpu.VMEM((R_ROWS, TILE), f32),
            dma((2,)), dma((2,)), dma, dma((2, INNER)), dma((2, INNER)),
            dma((g_count,)), dma((g_count,)), dma((r_count,)), dma((r_count,)),
        ]
        + [pltpu.VMEM(shape, f32) for shape in g_shapes + r_shapes],
        compiler_params=pltpu.CompilerParams(
            collective_id=0, has_side_effects=True, vmem_limit_bytes=51 << 20
        ),
        name="sketch",
    )(features, targets, small)


def predict_kernel(feat, weights_in, sketch_in, sketch_ref, weights_ref, predictions, guess, copy_sem, store_sem):
    copy = pltpu.make_async_copy(sketch_in, sketch_ref, copy_sem)
    copy.start()
    weights_ref[...] = weights_in[...]
    narrow = weights_in[...].astype(jnp.bfloat16)
    chunk = BLOCK // 8
    stores = []
    for c in range(8):
        rows = slice(c * chunk, (c + 1) * chunk)
        guess[rows, :] = dot(feat[rows, :], narrow).astype(jnp.bfloat16)
        where = pl.ds(c * chunk, chunk)
        store = pltpu.make_async_copy(guess.at[where], predictions.at[where], store_sem.at[c])
        store.start()
        stores.append(store)
    for store in stores:
        store.wait()
    copy.wait()


def predict(features, weights, sketch):
    vmem = pl.BlockSpec(memory_space=pltpu.VMEM)
    hbm = pl.BlockSpec(memory_space=pl.ANY)
    return pl.pallas_call(
        predict_kernel,
        out_shape=(
            jax.ShapeDtypeStruct((KEEP, F + K), jnp.bfloat16),
            jax.ShapeDtypeStruct((F, K), jnp.float32),
            jax.ShapeDtypeStruct((BLOCK, K), jnp.bfloat16),
        ),
        in_specs=[vmem, vmem, hbm],
        out_specs=(hbm, vmem, hbm),
        scratch_shapes=[
            pltpu.VMEM((BLOCK, K), jnp.bfloat16),
            pltpu.SemaphoreType.DMA,
            pltpu.SemaphoreType.DMA((8,)),
        ],
        compiler_params=pltpu.CompilerParams(vmem_limit_bytes=12 << 20),
        name="predict",
    )(features, weights, sketch)


def per_device(features, targets, signs, picks, routes):
    sketch, weights = sketch_and_weights(
        features,
        targets,
        jnp.concatenate([signs, picks, routes]).reshape((BLOCK + 2 * KEEP) // TILE, TILE),
    )
    return predict(features, weights, sketch)


def solution(mesh):
    both = ("outer", "inner")
    in_specs = (P(both, None), P(both, None), P(both), P(both), P(both))
    out_specs = (P(both, None), P(), P(both, None))
    return jax.shard_map(per_device, mesh=mesh, in_specs=in_specs, out_specs=out_specs, check_vma=False)
```

```python
import functools
import math

import jax
import jax.numpy as jnp
from jax import lax
from jax.experimental import pallas as pl
from jax.experimental.pallas import tpu as pltpu
from jax.sharding import PartitionSpec as P

F = 512
K = 256
BLOCK = 4096
KEEP = 1024
INNER = 32
NX, NC, NY, NZ = 4, 2, 4, 8
SECTION = KEEP // INNER
TILE = 128
G_BLOCKS = [(i, j) for i in range(4) for j in range(i, 4)]
R_BLOCKS = [(i, j) for i in range(4) for j in range(4, 6)]
G_ROWS = TILE * len(G_BLOCKS)
R_ROWS = TILE * len(R_BLOCKS)
MESH = pl.DeviceIdType.MESH

NN = (((1,), (0,)), ((), ()))
NT = (((1,), (1,)), ((), ()))
TN = (((0,), (0,)), ((), ()))


def dot(a, b, dims=NN, precision=None):
    return lax.dot_general(a, b, dims, precision=precision, preferred_element_type=jnp.float32)


def iota(shape, dim):
    return lax.broadcasted_iota(jnp.int32, shape, dim)


def parity_sign(bits):
    bits = bits ^ (bits >> 4)
    bits = bits ^ (bits >> 2)
    bits = bits ^ (bits >> 1)
    return (1 - 2 * (bits & 1)).astype(jnp.float32)


def position(inner):
    return inner // NZ, lax.rem(inner, NZ)


def order_picks(small_ref, upper_ref, coded_ref, factors_ref):
    first = BLOCK // TILE

    def row_of(first):
        return jnp.concatenate([small_ref[first + i : first + i + 1, :] for i in range(KEEP // TILE)], 1)

    picks = row_of(first)
    routes = row_of(first + KEEP // TILE)

    above = (iota((TILE, TILE), 0) < iota((TILE, TILE), 1)).astype(jnp.float32).astype(jnp.bfloat16)
    for q in range(KEEP // TILE):
        for p in range(KEEP // TILE):
            tile = above if p == q else jnp.full((TILE, TILE), float(p > q), jnp.bfloat16)
            upper_ref[q * TILE : (q + 1) * TILE, p * TILE : (p + 1) * TILE] = tile

    hot = (iota((INNER, KEEP), 0) == routes).astype(jnp.float32)
    before = dot(hot.astype(jnp.bfloat16), upper_ref[...])
    rank = jnp.sum(hot * before, axis=0, keepdims=True)
    place = routes * SECTION + rank.astype(jnp.int32)
    for n, part in enumerate((picks & (TILE - 1), picks >> 7)):
        coded_ref[n * TILE : (n + 1) * TILE, :] = jnp.broadcast_to(
            part.astype(jnp.float32), (TILE, KEEP)
        ).astype(jnp.bfloat16)

    rows = 2 * TILE

    @pl.loop(0, KEEP // rows)
    def _(c):
        at = pl.multiple_of(c * rows, rows)
        chosen = (iota((rows, KEEP), 0) + at == place).astype(jnp.float32).astype(jnp.bfloat16)
        found = dot(chosen, coded_ref[...], NT).astype(jnp.int32)
        low = found[:, :TILE] & iota((rows, TILE), 1)
        factors_ref[pl.ds(at, rows), :TILE] = parity_sign(low).astype(jnp.bfloat16)
        for bit in range(5):
            high = 1 - 2 * ((found[:, TILE:] >> bit) & 1)
            factors_ref[pl.ds(at, rows), (bit + 1) * TILE : (bit + 2) * TILE] = high.astype(jnp.float32).astype(jnp.bfloat16)


def fill_signs(signs_ref, flips_ref):
    for q in range(BLOCK // TILE):
        row = (2 * signs_ref[q : q + 1, :] - 1).astype(jnp.float32)
        flips_ref[:, q * TILE : (q + 1) * TILE] = jnp.broadcast_to(row, (16, TILE)).astype(jnp.bfloat16)


def fill_mixer(factors_ref, flips_ref, mixer_ref):
    rows = 64

    @pl.loop(0, KEEP // rows)
    def _(c):
        at = pl.multiple_of(c * rows, rows)
        here = factors_ref[pl.ds(at, rows), 0:TILE]
        gray = 0
        for step in range(BLOCK // TILE):
            if step:
                bit = (step & -step).bit_length() - 1
                gray ^= 1 << bit
                here = here * factors_ref[pl.ds(at, rows), (bit + 1) * TILE : (bit + 2) * TILE]
            flip = flips_ref[:, gray * TILE : (gray + 1) * TILE]
            flip = jnp.concatenate([flip] * (rows // 16), 0)
            mixer_ref[pl.ds(at, rows), gray * TILE : (gray + 1) * TILE] = here * flip


SIZES = {"core": NC, "plane": NX * NY, "z": NZ}


def flow_scratch(rows, stages):
    shapes, count = [], 0
    for kind, axis in stages:
        n = SIZES[axis]
        count += n - 1
        if kind == "scatter":
            rows //= n
            shapes.append((n - 1, rows, TILE))
        elif kind == "exchange":
            shapes.append((n, rows, TILE))
        else:
            rows *= n
    return shapes, count


class Flow:
    def __init__(self, own, total, first, rows, stages, landing, send, recv):
        self.own, self.total, self.at, self.rows = own, total, first, rows
        self.stages, self.landing, self.send, self.recv = list(stages), list(landing), send, recv
        self.slot = 0
        self.exchanges_left = sum(kind == "exchange" for kind, _ in stages)
        outer = lax.axis_index("outer")
        inner = lax.axis_index("inner")
        self.x, self.y = outer // NC, inner // NZ
        self.place = {"core": lax.rem(outer, NC), "plane": self.x * NY + self.y, "z": lax.rem(inner, NZ)}

    def device(self, axis, to):
        if axis == "core":
            return {"outer": self.x * NC + to}
        if axis == "plane":
            return {"outer": (to // NY) * NC + self.place["core"], "inner": lax.rem(to, NY) * NZ + self.place["z"]}
        return {"inner": self.y * NZ + to}

    def start(self):
        kind, axis = self.stages.pop(0)
        n, me = SIZES[axis], self.place[axis]
        buffer = None if kind == "gather" else self.landing.pop(0)
        copies = []
        for d in range(1, n):
            to = lax.rem(me + d, n)
            if kind == "scatter":
                piece = self.rows // n
                src = self.own.at[pl.ds(pl.multiple_of(self.at + to * piece, 8), piece)]
                dst = buffer.at[d - 1]
            elif kind == "exchange":
                src = self.own.at[pl.ds(pl.multiple_of(self.at, 8), self.rows)]
                dst = buffer.at[me]
            else:
                src = dst = self.total.at[pl.ds(pl.multiple_of(self.at, 8), self.rows)]
            copies.append(
                pltpu.make_async_remote_copy(
                    src_ref=src,
                    dst_ref=dst,
                    send_sem=self.send.at[self.slot],
                    recv_sem=self.recv.at[self.slot],
                    device_id=self.device(axis, to),
                    device_id_type=MESH,
                )
            )
            self.slot += 1
        for copy in copies:
            copy.start()
        self.flight = kind, axis, buffer, copies

    def finish(self):
        kind, axis, buffer, copies = self.flight
        n, me = SIZES[axis], self.place[axis]
        if kind == "exchange":
            buffer[me] = self.own[pl.ds(pl.multiple_of(self.at, 8), self.rows), :]
        for copy in copies:
            copy.wait()
        if kind == "scatter":
            self.rows //= n
            self.at = self.at + me * self.rows
            where = pl.ds(pl.multiple_of(self.at, 8), self.rows)
            terms = [self.own[where, :]] + [buffer[i] for i in range(n - 1)]
        elif kind == "exchange":
            where = pl.ds(pl.multiple_of(self.at, 8), self.rows)
            terms = [buffer[i] for i in range(n)]
        else:
            self.at = self.at - me * self.rows
            self.rows *= n
            return
        while len(terms) > 1:
            terms = [terms[i] + terms[i + 1] for i in range(0, len(terms), 2)]
        self.exchanges_left -= kind == "exchange"
        into = self.own if self.exchanges_left else self.total
        into[where, :] = terms[0]

    def step(self):
        if getattr(self, "flight", None):
            self.finish()
            self.flight = None
        if self.stages:
            self.start()

    def done(self):
        return not self.stages and self.flight is None


CORE = [("scatter", "core")]
PLANE = [("scatter", "plane"), ("exchange", "z"), ("gather", "plane")]
G_FLOWS = [(G_ROWS // NC, PLANE)]
R_FLOWS = [(R_ROWS // NC, PLANE)]


class Sum:
    def __init__(self, own, total, rows, flows, landing, send, recv):
        self.core = Flow(own, total, 0, rows, CORE + [("gather", "core")], landing[:1], send, recv)
        self.core.exchanges_left = 1
        self.flows, self.args = None, (own, total, rows, flows, landing[1:], send, recv)
        self.phase = 0

    def step(self):
        if self.phase == 0:
            self.core.step()
        elif self.phase == 1:
            self.core.finish()
            self.core.flight = None
            own, total, rows, flows, landing, send, recv = self.args
            at, base, self.flows = self.core.at, 2, []
            for size, stages in flows:
                shapes, count = flow_scratch(size, stages)
                used = [landing.pop(0) for _ in shapes]
                flow = Flow(own, total, at, size, stages, used, send, recv)
                flow.slot = base
                base += count
                at = at + size
                flow.step()
                self.flows.append(flow)
        elif not all(flow.done() for flow in self.flows):
            for flow in self.flows:
                if not flow.done():
                    flow.step()
            if all(flow.done() for flow in self.flows):
                self.core.step()
        else:
            self.core.step()
            self.finished = True
        self.phase += 1

    finished = False


def sum_scratch(rows, flows):
    shapes, count = flow_scratch(rows, CORE)
    count += 1
    for size, stages in flows:
        more, n = flow_scratch(size, stages)
        shapes, count = shapes + more, count + n
    return shapes, count


def thirds(a):
    high = a.astype(jnp.bfloat16)
    rest = a - high.astype(jnp.float32)
    middle = rest.astype(jnp.bfloat16)
    return high, middle, (rest - middle.astype(jnp.float32)).astype(jnp.bfloat16)


def dot_exact(a, b):
    ah, am, al = thirds(a)
    bh, bm, bl = thirds(b)
    return dot(jnp.concatenate([ah, ah, am, am, ah, al], 1), jnp.concatenate([bh, bm, bh, bm, bl, bh], 0))


def invert(block):
    lane = iota((8, TILE), 1)
    sub = iota((8, TILE), 0)

    def spread(v, j):
        return jnp.broadcast_to(v[:, j : j + 1], (8, TILE))

    def down(v, i):
        return jnp.broadcast_to(v[i : i + 1, :], (8, TILE))

    v = [block[8 * i : 8 * i + 8, :] for i in range(16)]
    for g in range(16):
        base = 8 * g
        now = v[g]
        cols = [spread(now, base + j) for j in range(8)]
        for s in range(8):
            over = 1.0 / down(cols[s], s)
            mult = jnp.where(sub == s, 0.0, cols[s])
            for j in range(s + 1, 8):
                pivot = down(cols[j], s) * over
                cols[j] = jnp.where(sub == s, pivot, cols[j] - mult * pivot)
            row = jnp.where(lane == base + s, 1.0, down(now, s)) * over
            now = jnp.where(sub == s, row, jnp.where(lane == base + s, 0.0, now) - mult * row)
        rows = [down(now, j) for j in range(8)]
        panel = (lane >= base) & (lane < base + 8)
        new = []
        for i in range(16):
            if i == g:
                new.append(now)
                continue
            p = [spread(v[i], base + j) * rows[j] for j in range(8)]
            p = ((p[0] + p[1]) + (p[2] + p[3])) + ((p[4] + p[5]) + (p[6] + p[7]))
            new.append(jnp.where(panel, 0.0, v[i]) - p)
        v = new
    return jnp.concatenate(v, 0)


def fill_kron(kron):
    a, b = iota((TILE, TILE), 0), iota((TILE, TILE), 1)
    sign = parity_sign((a // SECTION) & (b // SECTION))
    tile = jnp.where((a ^ b) & (SECTION - 1) == 0, sign, 0.0)
    tiles = [tile.astype(jnp.bfloat16), (-tile).astype(jnp.bfloat16)]
    for q in range(KEEP // TILE):
        for p in range(KEEP // TILE):
            kron[q * TILE : (q + 1) * TILE, p * TILE : (p + 1) * TILE] = tiles[(q & p).bit_count() & 1]


EARLY = {(0, 0)}


def sketch_kernel(
    features, targets, small_ref,
    sketch_hbm, weights_ref,
    feat, targ, upper, coded, factors, flips, mixer,
    out_f, out_k, in_f, in_k, sketch, work, inverse, g_own, g_total, r_own, r_total,
    load_sem, own_sem, store_sem, send_sem, recv_sem, g_send, g_recv, r_send, r_recv, *landing
):
    outer = lax.axis_index("outer")
    me = lax.axis_index("inner")
    x, core = outer // NC, lax.rem(outer, NC)
    y, z = position(me)

    loads = [
        pltpu.make_async_copy(features, feat, load_sem.at[0]),
        pltpu.make_async_copy(targets, targ, load_sem.at[1]),
    ]
    for load in loads:
        load.start()

    barrier = pltpu.get_barrier_semaphore()

    @pl.loop(1, INNER)
    def _(d):
        pl.semaphore_signal(barrier, inc=1, device_id={"inner": lax.rem(me + d, INNER)}, device_id_type=MESH)

    pl.semaphore_signal(barrier, inc=1, device_id={"outer": x * NC + 1 - core}, device_id_type=MESH)

    @pl.loop(1, NX)
    def _(d):
        @pl.loop(0, NY)
        def _(row):
            pl.semaphore_signal(
                barrier,
                inc=1,
                device_id={"outer": lax.rem(x + d, NX) * NC + core, "inner": row * NZ + z},
                device_id_type=MESH,
            )

    order_picks(small_ref, upper, coded, factors)
    fill_signs(small_ref, flips)
    fill_mixer(factors, flips, mixer)
    pl.semaphore_wait(barrier, INNER - 1 + 1 + (NX - 1) * NY)

    def section(ref, d):
        return ref.at[pl.ds(pl.multiple_of(d * SECTION, SECTION), SECTION)]

    pairs = [(feat, out_f, in_f), (targ, out_k, in_k)]

    def exchange(kind, to, source):
        _, out, into = pairs[kind]
        return pltpu.make_async_remote_copy(
            src_ref=section(out, to),
            dst_ref=section(into, source),
            send_sem=send_sem.at[kind, to],
            recv_sem=recv_sem.at[kind, source],
            device_id={"inner": to},
            device_id_type=MESH,
        )

    span = NZ * SECTION

    def keep(kind, c):
        data, out, _ = pairs[kind]
        at = pl.multiple_of(lax.rem(y + c + 1, NY) * span, span)
        kept = dot(mixer[pl.ds(at, span), :], data[...])
        out[pl.ds(at, span), :] = (kept * (1.0 / 64)).astype(jnp.bfloat16)

    def send(kind, c):
        row = lax.rem(y + c + 1, NY)

        @pl.loop(0, NZ)
        def _(i):
            to = row * NZ + lax.rem(me + i + 1, NZ)

            @pl.when(to != me)
            def _():
                exchange(kind, to, me).start()

    def make(kind):
        loads[kind].wait()
        early = [c for c in range(NY) if (kind, c) in EARLY]
        if early:
            assert early == list(range(len(early)))

            @pl.loop(0, len(early))
            def _(c):
                keep(kind, c)
                send(kind, c)

        @pl.loop(len(early), NY)
        def _(c):
            keep(kind, c)

    def send_rest(kind):
        late = [c for c in range(NY) if (kind, c) not in EARLY]

        @pl.loop(late[0], NY)
        def _(c):
            send(kind, c)

    def arrive(kind):
        own[kind].wait()

        @pl.loop(1, INNER)
        def _(i):
            s = lax.rem(me + i, INNER)
            exchange(kind, s, s).wait()

    def mix(kind):
        first, width = ((0, F), (F, K))[kind]
        into = pairs[kind][2]

        @pl.loop(0, KEEP // 256)
        def _(c):
            at = pl.multiple_of(c * 256, 256)
            mixed = dot(upper[pl.ds(at, 256), :], into[...])
            sketch[pl.ds(at, 256), first : first + width] = (mixed * (1.0 / math.sqrt(INNER))).astype(jnp.bfloat16)

    def eliminate(b, columns):
        at = b * TILE
        pivot = dot_exact(inverse[b], work[at : at + TILE, columns])
        for first, last in ((0, at), (at + TILE, F)):
            if first < last:
                work[first:last, columns] = work[first:last, columns] - dot_exact(
                    work[first:last, at : at + TILE], pivot
                )
        work[at : at + TILE, columns] = pivot

    count = len(landing) - len(sum_scratch(R_ROWS, R_FLOWS)[0])
    g = Sum(g_own, g_total, G_ROWS, G_FLOWS, list(landing[:count]), g_send, g_recv)
    r = Sum(r_own, r_total, R_ROWS, R_FLOWS, list(landing[count:]), r_send, r_recv)

    make(0)
    for i in (0, 2):
        rows = dot(out_f[:, i * TILE : (i + 2) * TILE], out_f[:, i * TILE :], TN)
        for n, (p, q) in enumerate(G_BLOCKS):
            if p in (i, i + 1):
                g_own[n * TILE : (n + 1) * TILE, :] = rows[(p - i) * TILE : (p - i + 1) * TILE, (q - i) * TILE : (q - i + 1) * TILE]
    g.step()
    fill_kron(upper)
    g.step()
    make(1)
    own = [
        pltpu.make_async_copy(section(out_f, me), section(in_f, me), own_sem.at[0]),
        pltpu.make_async_copy(section(out_k, me), section(in_k, me), own_sem.at[1]),
    ]
    for copy in own:
        copy.start()
    for i in (0, 2):
        rows = dot(out_f[:, i * TILE : (i + 2) * TILE], out_k[...], TN)
        for n, (p, q) in enumerate(R_BLOCKS):
            if p in (i, i + 1):
                r_own[n * TILE : (n + 1) * TILE, :] = rows[(p - i) * TILE : (p - i + 1) * TILE, (q - 4) * TILE : (q - 3) * TILE]
    r.step()
    g.step()
    r.step()
    g.step()
    r.step()
    send_rest(0)
    send_rest(1)
    g.step()
    r.step()

    def unpack(half):
        for n in range(half * len(G_BLOCKS) // 2, (half + 1) * len(G_BLOCKS) // 2):
            i, j = G_BLOCKS[n]
            tile = g_total[n * TILE : (n + 1) * TILE, :]
            work[i * TILE : (i + 1) * TILE, j * TILE : (j + 1) * TILE] = tile
            if i != j:
                work[j * TILE : (j + 1) * TILE, i * TILE : (i + 1) * TILE] = tile.T

    pl.when(core == 0)(functools.partial(unpack, 0))
    pl.when(core == 1)(functools.partial(unpack, 1))
    g.step()
    assert g.finished
    pl.when(core == 0)(functools.partial(unpack, 1))
    pl.when(core == 1)(functools.partial(unpack, 0))
    targets_at = slice(F, F + K)
    for b in range(F // TILE):
        at = b * TILE
        inverse[b] = invert(work[at : at + TILE, at : at + TILE])
        if b < 3:
            eliminate(b, slice(at + TILE, F))
        if b == 0:
            r.step()
        if b == 1:
            r.step()
            assert r.finished
            for n, (i, j) in enumerate(R_BLOCKS):
                work[i * TILE : (i + 1) * TILE, j * TILE : (j + 1) * TILE] = r_total[n * TILE : (n + 1) * TILE, :]
            eliminate(0, targets_at)
        if b:
            eliminate(b, targets_at)
    weights_ref[...] = work[:, targets_at]
    for kind in (0, 1):
        arrive(kind)
        mix(kind)
    store = pltpu.make_async_copy(sketch, sketch_hbm, store_sem)
    store.start()
    store.wait()


def sketch_and_weights(features, targets, small):
    vmem = pl.BlockSpec(memory_space=pltpu.VMEM)
    hbm = pl.BlockSpec(memory_space=pl.ANY)
    f32, bf16 = jnp.float32, jnp.bfloat16
    dma = pltpu.SemaphoreType.DMA
    g_shapes, g_count = sum_scratch(G_ROWS, G_FLOWS)
    r_shapes, r_count = sum_scratch(R_ROWS, R_FLOWS)
    return pl.pallas_call(
        sketch_kernel,
        out_shape=(
            jax.ShapeDtypeStruct((KEEP, F + K), bf16),
            jax.ShapeDtypeStruct((F, K), f32),
        ),
        in_specs=[hbm, hbm, vmem],
        out_specs=(hbm, vmem),
        scratch_shapes=[
            pltpu.VMEM((BLOCK, F), bf16),
            pltpu.VMEM((BLOCK, K), bf16),
            pltpu.VMEM((KEEP, KEEP), bf16),
            pltpu.VMEM((2 * TILE, KEEP), bf16),
            pltpu.VMEM((KEEP, 6 * TILE), bf16),
            pltpu.VMEM((16, BLOCK), bf16),
            pltpu.VMEM((KEEP, BLOCK), bf16),
            pltpu.VMEM((KEEP, F), bf16),
            pltpu.VMEM((KEEP, K), bf16),
            pltpu.VMEM((KEEP, F), bf16),
            pltpu.VMEM((KEEP, K), bf16),
            pltpu.VMEM((KEEP, F + K), bf16),
            pltpu.VMEM((F, F + K), f32),
            pltpu.VMEM((F // TILE, TILE, TILE), f32),
            pltpu.VMEM((G_ROWS, TILE), f32),
            pltpu.VMEM((G_ROWS, TILE), f32),
            pltpu.VMEM((R_ROWS, TILE), f32),
            pltpu.VMEM((R_ROWS, TILE), f32),
            dma((2,)), dma((2,)), dma, dma((2, INNER)), dma((2, INNER)),
            dma((g_count,)), dma((g_count,)), dma((r_count,)), dma((r_count,)),
        ]
        + [pltpu.VMEM(shape, f32) for shape in g_shapes + r_shapes],
        compiler_params=pltpu.CompilerParams(
            collective_id=0, has_side_effects=True, vmem_limit_bytes=51 << 20
        ),
        name="sketch",
    )(features, targets, small)


def predict_kernel(feat, weights_in, sketch_in, sketch_ref, weights_ref, predictions, guess, copy_sem, store_sem):
    copy = pltpu.make_async_copy(sketch_in, sketch_ref, copy_sem)
    copy.start()
    weights_ref[...] = weights_in[...]
    narrow = weights_in[...].astype(jnp.bfloat16)
    chunk = BLOCK // 8
    stores = []
    for c in range(8):
        rows = slice(c * chunk, (c + 1) * chunk)
        guess[rows, :] = dot(feat[rows, :], narrow).astype(jnp.bfloat16)
        where = pl.ds(c * chunk, chunk)
        store = pltpu.make_async_copy(guess.at[where], predictions.at[where], store_sem.at[c])
        store.start()
        stores.append(store)
    for store in stores:
        store.wait()
    copy.wait()


def predict(features, weights, sketch):
    vmem = pl.BlockSpec(memory_space=pltpu.VMEM)
    hbm = pl.BlockSpec(memory_space=pl.ANY)
    return pl.pallas_call(
        predict_kernel,
        out_shape=(
            jax.ShapeDtypeStruct((KEEP, F + K), jnp.bfloat16),
            jax.ShapeDtypeStruct((F, K), jnp.float32),
            jax.ShapeDtypeStruct((BLOCK, K), jnp.bfloat16),
        ),
        in_specs=[vmem, vmem, hbm],
        out_specs=(hbm, vmem, hbm),
        scratch_shapes=[
            pltpu.VMEM((BLOCK, K), jnp.bfloat16),
            pltpu.SemaphoreType.DMA,
            pltpu.SemaphoreType.DMA((8,)),
        ],
        compiler_params=pltpu.CompilerParams(vmem_limit_bytes=12 << 20),
        name="predict",
    )(features, weights, sketch)


def per_device(features, targets, signs, picks, routes):
    sketch, weights = sketch_and_weights(
        features,
        targets,
        jnp.concatenate([signs, picks, routes]).reshape((BLOCK + 2 * KEEP) // TILE, TILE),
    )
    return predict(features, weights, sketch)


def solution(mesh):
    both = ("outer", "inner")
    in_specs = (P(both, None), P(both, None), P(both), P(both), P(both))
    out_specs = (P(both, None), P(), P(both, None))
    return jax.shard_map(per_device, mesh=mesh, in_specs=in_specs, out_specs=out_specs, check_vma=False)
```
